256 devices in a mesh: samp: 32 (over x, z_hi, y), par: 8 (over z_lo, core).
Axes of the slice: x: 4, y: 4, z: 8 (z_hi: 2, z_lo: 4; z = z_hi * 4 + z_lo), core: 2. Of those that a mesh axis runs over, the one named last changes fastest.
Arguments:
- spins: int32 [256, 100], P('samp'), may hold values from -1 to 1, as said below
- embed: float32 [4, 64], replicated, may hold values from -3 to 3
- position: float32 [25, 64], replicated, may hold values from -3 to 3
- w_first: bfloat16 [64, 256], P(None, 'par'), may hold values from -0.75 to 0.75
- bias_first: float32 [256], P('par'), may hold values from -3 to 3
- readout: float32 [256], P('par'), may hold values from -1.2 to 1.2
- other_grads: bfloat16 [256, 32768], P('samp', 'par'), may hold values from -3 to 3
- energies: float32 [256], replicated, may hold values from -6 to 6
- shift: float32 [1], replicated, may hold values from 0.5 to 2
Outputs:
- coeffs: float32 [256], P('samp')
- update: float32 [64, 256], P(None, 'par')
- update_rest: float32 [32768], P('par')
The draws below stay inside these ranges and needn't reach their ends.
Inputs may be any that keep to these rules, and one draw needn't show every extreme that they name: `spins`: every entry is -1 or +1.
All inputs are finite; a program needn't handle non-finite values.
Results may differ from the reference program's by a relative error of at most 0.0054.
The reference program's roundings to bfloat16 on the way (of `hidden` and `centered`) count: a program that leaves them out, or rounds other values in their place, can miss the bound.
Values may be sent and summed in bfloat16 or wider, within the bound.
A program may use at most 64 MiB of HBM per device.

```python
import math
import jax
import jax.numpy as jnp
from jax import lax

LSIDE = 10
PATCH = 2
SITES = 100
PATCHES = 25
PDIM = 4
D = 64
FF = 256
SAMPLES = 256
OTHER = 32768


def draw_spins(key, part):
    key = jax.random.fold_in(key, 7)
    return 2 * jax.random.randint(key, (SAMPLES, SITES), 0, 2).astype(jnp.int32) - 1


def block_levels(own_key, extent, cuts, least, top_value):
    factor_of, own = 1.0, jax.random.fold_in(own_key, 6)
    for dim, blocks in cuts:
        draws = jnp.exp(jax.random.uniform(jax.random.fold_in(own, dim), (blocks,), jnp.float32, least / len(cuts), top_value / len(cuts)))
        factor_of = factor_of * jnp.repeat(draws, extent[dim] // blocks).reshape([-1 if axis == dim else 1 for axis in range(len(extent))])
    return factor_of


def scatter_about(rng, extent, width, limit, split=(), kind=jnp.bfloat16):
    result = width * jax.random.normal(rng, extent, jnp.float32)
    if split:
        result = result * block_levels(rng, extent, split, -0.22, 0.18)
    return jnp.clip(result, -limit, limit).astype(kind)


def setup_inputs(seed: int = 0) -> dict:
    seeds = jax.random.split(jax.random.key(seed), 10)
    return {
        "spins": draw_spins(jax.random.fold_in(seeds[9], 71), 0),
        "embed": scatter_about(seeds[1], (PDIM, D), PDIM ** -0.5, 3.0, (), jnp.float32),
        "position": scatter_about(seeds[2], (PATCHES, D), 0.5, 3.0, (), jnp.float32),
        "w_first": scatter_about(seeds[3], (D, FF), D ** -0.5, 0.75, ((1, 8),)),
        "bias_first": scatter_about(seeds[4], (FF,), 0.5, 3.0, ((0, 8),), jnp.float32),
        "readout": scatter_about(seeds[5], (FF,), 0.2, 1.2, ((0, 8),), jnp.float32),
        "other_grads": scatter_about(seeds[6], (SAMPLES, OTHER), 0.5, 3.0, ((0, 32), (1, 8))),
        "energies": scatter_about(seeds[7], (SAMPLES,), 1.0, 6.0, (), jnp.float32),
        "shift": jnp.clip(jnp.exp(jax.random.uniform(seeds[8], (1,), jnp.float32, math.log(0.5), math.log(2.0))), 0.5, 2.0),
    }


def reference(spins, embed, position, w_first, bias_first, readout, other_grads, energies, shift):
    count = spins.shape[0]
    sides = LSIDE // PATCH
    blocks = spins.reshape(count, sides, PATCH, sides, PATCH).transpose(0, 1, 3, 2, 4)
    patches = blocks.reshape(count, PATCHES, PDIM).astype(jnp.float32)
    hidden = (jnp.einsum('spk,kd->spd', patches, embed, precision=lax.Precision.HIGHEST) + position).astype(jnp.bfloat16)
    act = jnp.einsum('spd,df->spf', hidden.astype(jnp.float32), w_first.astype(jnp.float32), precision=lax.Precision.HIGHEST) + bias_first
    slope = readout * jnp.tanh(act)
    grads = jnp.einsum('spd,spf->sdf', hidden.astype(jnp.float32), slope, precision=lax.Precision.HIGHEST)
    joined = jnp.concatenate([grads.reshape(count, D * FF), other_grads.astype(jnp.float32)], axis=1)
    scale = 1.0 / math.sqrt(SAMPLES)
    centered = ((joined - lax.optimization_barrier(jnp.sum(joined, axis=0)) / SAMPLES) * scale).astype(jnp.bfloat16)
    gram = lax.dot_general(centered.astype(jnp.float32), centered.astype(jnp.float32), (((1,), (1,)), ((), ())), preferred_element_type=jnp.float32)
    matrix = gram + shift[0] * jnp.eye(SAMPLES, dtype=jnp.float32)
    lower = jnp.linalg.cholesky(matrix)
    target = energies - jnp.sum(energies) / SAMPLES
    coeffs = jax.scipy.linalg.cho_solve((lower, True), target)
    full = jnp.dot(coeffs, centered.astype(jnp.float32), precision=lax.Precision.HIGHEST)
    return (coeffs, full[:D * FF].reshape(D, FF), full[D * FF:])
```

```python
import functools

import jax
import jax.numpy as jnp
from jax import lax
from jax.experimental import pallas as pl
from jax.experimental.pallas import tpu as pltpu
from jax.sharding import PartitionSpec as P

MESH = pl.DeviceIdType.MESH
HI = lax.Precision.HIGHEST
F32 = jnp.float32
BF16 = jnp.bfloat16

LSIDE = 10
PATCHES = 25
D = 64
SAMPLES = 256
OWN = 8
FOWN = 32
NSAMP = 32
NPAR = 8
NX, NZH, NY = 4, 2, 4
ROWS = PATCHES * OWN


def place():
    samp = lax.axis_index("samp")
    par = lax.axis_index("par")
    x, zh, y = samp // 8, (samp // 4) % 2, samp % 4
    zl, core = par // 2, par % 2
    return samp, par, x, zh, y, zl, core


def local_derivatives(spins_ref, embed_ref, position_ref, w_ref, bias_ref, readout_ref, spin_pad, table, w_pad, slope_pad):
    spin_pad[...] = jnp.zeros_like(spin_pad)
    spin_pad[:, 0:100] = spins_ref[...].astype(F32)
    table[0:4, 0:D] = embed_ref[...]
    table[0:4, D : 2 * D] = embed_ref[...]
    table[8 : 8 + PATCHES, 0:D] = position_ref[...]
    table[8 : 8 + PATCHES, D : 2 * D] = position_ref[...]
    site = lax.broadcasted_iota(jnp.int32, (128, 128), 0)
    line = (site * 205) >> 11
    kind = (line & 1) * 2 + ((site - line * 10) & 1)
    spread = jnp.where(
        kind == 0,
        table[0:1, :],
        jnp.where(kind == 1, table[1:2, :], jnp.where(kind == 2, table[2:3, :], table[3:4, :])),
    )
    site = lax.broadcasted_iota(jnp.int32, (ROWS, 128), 1)
    line = (site * 205) >> 11
    patch = (line >> 1) * 5 + ((site - line * 10) >> 1)
    row_patch = lax.broadcasted_iota(jnp.int32, (ROWS, 128), 0) >> 3
    own_spins = jnp.concatenate([spin_pad[...]] * PATCHES, axis=0)
    picked = jnp.where(patch == row_patch, own_spins, 0.0)
    offsets = jnp.concatenate(
        [jnp.broadcast_to(table[8 + p : 9 + p, :], (OWN, 128)) for p in range(PATCHES)], axis=0
    )
    hidden = (jnp.dot(picked, spread, precision=HI, preferred_element_type=F32) + offsets).astype(BF16)
    w_pad[...] = jnp.zeros_like(w_pad)
    w_pad[0:D, :] = w_ref[...].astype(F32)
    act = jnp.dot(hidden, w_pad[...].astype(BF16), preferred_element_type=F32) + bias_ref[...]
    slope_pad[...] = jnp.zeros_like(slope_pad)
    slope_pad[0:ROWS, 0:FOWN] = readout_ref[...] * jnp.tanh(act)
    slope_t = jnp.transpose(slope_pad[...])[0:FOWN, :]
    sample = lax.broadcasted_iota(jnp.int32, (OWN, 256), 0)
    row_sample = lax.broadcasted_iota(jnp.int32, (OWN, 256), 1) & 7
    same = (sample == row_sample)[None]
    left = jnp.where(same, jnp.broadcast_to(slope_t[:, None, :], (FOWN, OWN, 256)), 0.0)
    left = left.reshape(FOWN * OWN, 256)
    right = jnp.concatenate([hidden.astype(F32), jnp.zeros((256 - ROWS, 128), F32)], axis=0)
    return jnp.dot(left, right, precision=HI, preferred_element_type=F32)


def gram_kernel(
    spins_ref, embed_ref, position_ref, w_ref, bias_ref, readout_ref, other_ref,
    gram_ref, cent_ref,
    spin_pad, table, w_pad, slope_pad, sbuf, rbuf, cbuf, pair_out, pair_in, half, xy_in, z_in, send_sem, recv_sem,
):
    samp, par, x, zh, y, zl, core = place()
    q = x * 4 + y
    z = zh * 4 + zl
    mate = zl * 2 + (1 - core)

    def samp_peer(k):
        return (lax.rem(samp + k, NSAMP), par)

    def xy_peer(k):
        nx = lax.rem(x + k // 4, 4)
        ny = lax.rem(y + k % 4, 4)
        return nx * 4 + ny, (nx * 8 + zh * 4 + ny, par)

    def z_peer(k):
        nz = lax.rem(z + k, 8)
        return nz, (x * 8 + (nz // 4) * 4 + y, (nz % 4) * 2 + core)

    barrier = pltpu.get_barrier_semaphore()
    greeted = 0
    for k in range(1, NSAMP):
        pl.semaphore_signal(barrier, inc=1, device_id=samp_peer(k), device_id_type=MESH)
        greeted += 1
    for k in (1, 2, 3, 5, 6, 7):
        pl.semaphore_signal(barrier, inc=1, device_id=z_peer(k)[1], device_id_type=MESH)
        greeted += 1
    pl.semaphore_signal(barrier, inc=1, device_id=(samp, mate), device_id_type=MESH)
    greeted += 1

    grads = local_derivatives(
        spins_ref, embed_ref, position_ref, w_ref, bias_ref, readout_ref, spin_pad, table, w_pad, slope_pad
    )
    lane = lax.broadcasted_iota(jnp.int32, (256, 128), 1)
    high = grads.astype(BF16).astype(F32)
    terms = jnp.where(lane < D, high, grads - high)
    for j in range(NSAMP):
        sbuf[j] = jnp.concatenate(
            [other_ref[:, 128 * j : 128 * (j + 1)].astype(F32), terms[8 * j : 8 * (j + 1), :]], axis=0
        ).astype(BF16)

    pl.semaphore_wait(barrier, greeted)

    for k in range(1, NSAMP):
        to = samp_peer(k)
        pltpu.make_async_remote_copy(
            src_ref=sbuf.at[to[0]], dst_ref=rbuf.at[samp], send_sem=send_sem.at[0], recv_sem=recv_sem.at[0],
            device_id=to, device_id_type=MESH,
        ).start()
    rbuf[samp] = sbuf[samp]
    most = rbuf.at[pl.ds(0, NSAMP - 1)]
    pltpu.make_async_copy(most, most, recv_sem.at[0]).wait()

    got = rbuf[...].astype(F32)
    others = got[:, 0:8, :].reshape(SAMPLES, 128)
    pair = got[:, 8:16, :].reshape(SAMPLES, 128)
    layer = jnp.where(lane < D, pair + pltpu.roll(pair, D, 1), 0.0)
    for n, joined in enumerate((others, layer)):
        mean = jnp.sum(joined, axis=0, keepdims=True) / SAMPLES
        cbuf[:, 128 * n : 128 * (n + 1)] = ((joined - mean) * 0.0625).astype(BF16)
    cent_ref[...] = cbuf[...]

    def rows_of(c):
        return lax.dot_general(
            cbuf[pl.ds(pl.multiple_of(c * 128, 128), 128), :], cbuf[...], (((1,), (1,)), ((), ())),
            preferred_element_type=F32,
        )

    pair_out[...] = rows_of(1 - core)
    swap = pltpu.make_async_remote_copy(
        src_ref=pair_out, dst_ref=pair_in, send_sem=send_sem.at[1], recv_sem=recv_sem.at[1],
        device_id=(samp, mate), device_id_type=MESH,
    )
    swap.start()
    own = rows_of(core)
    swap.wait_recv()
    half[...] = (own + pair_in[...]).reshape(16, 8, 256)

    for k in range(1, 16):
        nq, to = xy_peer(k)
        pltpu.make_async_remote_copy(
            src_ref=half.at[nq], dst_ref=xy_in.at[q], send_sem=send_sem.at[2], recv_sem=recv_sem.at[2],
            device_id=to, device_id_type=MESH,
        ).start()
    xy_in[q] = half[q]
    most = xy_in.at[pl.ds(0, 15)]
    pltpu.make_async_copy(most, most, recv_sem.at[2]).wait()
    z_in[z] = jnp.sum(xy_in[...], axis=0)

    for k in range(1, 8):
        to = z_peer(k)[1]
        pltpu.make_async_remote_copy(
            src_ref=z_in.at[z], dst_ref=z_in.at[z], send_sem=send_sem.at[3], recv_sem=recv_sem.at[3],
            device_id=to, device_id_type=MESH,
        ).start()
    most = z_in.at[pl.ds(0, 7)]
    pltpu.make_async_copy(most, most, recv_sem.at[3]).wait()
    mine = core * 16 + q
    gram_ref[mine] = jnp.sum(z_in[...], axis=0)

    for k in range(1, 16):
        to = xy_peer(k)[1]
        pltpu.make_async_remote_copy(
            src_ref=gram_ref.at[mine], dst_ref=gram_ref.at[mine], send_sem=send_sem.at[4], recv_sem=recv_sem.at[4],
            device_id=to, device_id_type=MESH,
        ).start()
    most = gram_ref.at[pl.ds(core * 16, 15)]
    pltpu.make_async_copy(most, most, recv_sem.at[4]).wait()
    own_half = gram_ref.at[pl.ds(core * 16, 16)]
    swap = pltpu.make_async_remote_copy(
        src_ref=own_half, dst_ref=own_half, send_sem=send_sem.at[5], recv_sem=recv_sem.at[5],
        device_id=(samp, mate), device_id_type=MESH,
    )
    swap.start()
    swap.wait_recv()

    for ref, n, size in ((sbuf, 0, 31), (pair_out, 1, None), (half, 2, 15), (z_in, 3, 7), (gram_ref, 4, 15), (gram_ref, 5, 16)):
        part = ref if size is None else ref.at[pl.ds(0, size)]
        pltpu.make_async_copy(part, part, send_sem.at[n]).wait()


def gather_kernel(row_ref, rest_ref, layer_ref, recv, send_sem, recv_sem):
    samp, par = lax.axis_index("samp"), lax.axis_index("par")
    barrier = pltpu.get_barrier_semaphore()
    for k in range(1, NSAMP):
        pl.semaphore_signal(barrier, inc=1, device_id=(lax.rem(samp + k, NSAMP), par), device_id_type=MESH)
    recv[samp] = row_ref[...]
    pl.semaphore_wait(barrier, NSAMP - 1)
    for k in range(1, NSAMP):
        pltpu.make_async_remote_copy(
            src_ref=row_ref, dst_ref=recv.at[samp], send_sem=send_sem, recv_sem=recv_sem,
            device_id=(lax.rem(samp + k, NSAMP), par), device_id_type=MESH,
        ).start()
    most = recv.at[pl.ds(0, NSAMP - 1)]
    pltpu.make_async_copy(most, most, recv_sem).wait()
    got = recv[...]
    rest_ref[...] = got[:, 0, :]
    layer_ref[...] = jnp.transpose(got[:, 1, :])[0:D, :]
    pltpu.make_async_copy(most, most, send_sem).wait()


def per_device(spins, embed, position, w_first, bias_first, readout, other_grads, energies, shift):
    vmem = pl.BlockSpec(memory_space=pltpu.VMEM)
    gram, cent = pl.pallas_call(
        gram_kernel,
        out_shape=(jax.ShapeDtypeStruct((32, 8, 256), F32), jax.ShapeDtypeStruct((256, 256), BF16)),
        in_specs=[vmem] * 7,
        out_specs=(vmem, vmem),
        scratch_shapes=[
            pltpu.VMEM((8, 128), F32),
            pltpu.VMEM((40, 128), F32),
            pltpu.VMEM((128, FOWN), F32),
            pltpu.VMEM((256, 128), F32),
            pltpu.VMEM((NSAMP, 16, 128), BF16),
            pltpu.VMEM((NSAMP, 16, 128), BF16),
            pltpu.VMEM((256, 256), BF16),
            pltpu.VMEM((128, 256), F32),
            pltpu.VMEM((128, 256), F32),
            pltpu.VMEM((16, 8, 256), F32),
            pltpu.VMEM((16, 8, 256), F32),
            pltpu.VMEM((8, 8, 256), F32),
            pltpu.SemaphoreType.DMA((6,)),
            pltpu.SemaphoreType.DMA((6,)),
        ],
        compiler_params=pltpu.CompilerParams(
            collective_id=0, has_side_effects=True, vmem_limit_bytes=32 * 2**20
        ),
        name="gram",
    )(spins, embed, position, w_first, bias_first.reshape(1, -1), readout.reshape(1, -1), other_grads)
    matrix = gram.reshape(SAMPLES, SAMPLES) + shift[0] * jnp.eye(SAMPLES, dtype=F32)
    lower = jnp.linalg.cholesky(matrix)
    target = energies - jnp.sum(energies) / SAMPLES
    solved = jax.scipy.linalg.cho_solve((lower, True), target)
    coeffs = lax.dynamic_slice_in_dim(solved, lax.axis_index("samp") * OWN, OWN, 0)
    row = jnp.dot(solved, cent.astype(F32), precision=HI).reshape(2, 128)
    rest, layer = pl.pallas_call(
        gather_kernel,
        out_shape=(jax.ShapeDtypeStruct((NSAMP, 128), F32), jax.ShapeDtypeStruct((D, FOWN), F32)),
        in_specs=[vmem],
        out_specs=(vmem, vmem),
        scratch_shapes=[
            pltpu.VMEM((NSAMP, 2, 128), F32),
            pltpu.SemaphoreType.DMA,
            pltpu.SemaphoreType.DMA,
        ],
        compiler_params=pltpu.CompilerParams(
            collective_id=1, has_side_effects=True, vmem_limit_bytes=32 * 2**20
        ),
        name="gather",
    )(row)
    return (coeffs, layer, rest.reshape(-1))


def solution(mesh):
    return jax.shard_map(
        per_device,
        mesh=mesh,
        in_specs=(
            P("samp", None), P(), P(), P(None, "par"), P("par"), P("par"), P("samp", "par"), P(), P(),
        ),
        out_specs=(P("samp"), P(None, "par"), P("par")),
        check_vma=False,
    )
```

```python
import functools

import jax
import jax.numpy as jnp
from jax import lax
from jax.experimental import pallas as pl
from jax.experimental.pallas import tpu as pltpu
from jax.sharding import PartitionSpec as P

MESH = pl.DeviceIdType.MESH
HI = lax.Precision.HIGHEST
F32 = jnp.float32
BF16 = jnp.bfloat16

LSIDE = 10
PATCHES = 25
D = 64
SAMPLES = 256
OWN = 8
FOWN = 32
NSAMP = 32
NPAR = 8
NX, NZH, NY = 4, 2, 4
PANEL = 16
ROWS = PATCHES * OWN


def place():
    samp = lax.axis_index("samp")
    par = lax.axis_index("par")
    x, zh, y = samp // 8, (samp // 4) % 2, samp % 4
    zl, core = par // 2, par % 2
    return samp, par, x, zh, y, zl, core


def local_derivatives(spins_ref, embed_ref, position_ref, w_ref, bias_ref, readout_ref, spin_pad, table, w_pad, slope_pad):
    spin_pad[...] = jnp.zeros_like(spin_pad)
    spin_pad[:, 0:100] = spins_ref[...].astype(F32)
    table[0:4, 0:D] = embed_ref[...]
    table[0:4, D : 2 * D] = embed_ref[...]
    table[8 : 8 + PATCHES, 0:D] = position_ref[...]
    table[8 : 8 + PATCHES, D : 2 * D] = position_ref[...]
    site = lax.broadcasted_iota(jnp.int32, (128, 128), 0)
    line = (site * 205) >> 11
    kind = (line & 1) * 2 + ((site - line * 10) & 1)
    spread = jnp.where(
        kind == 0,
        table[0:1, :],
        jnp.where(kind == 1, table[1:2, :], jnp.where(kind == 2, table[2:3, :], table[3:4, :])),
    )
    site = lax.broadcasted_iota(jnp.int32, (ROWS, 128), 1)
    line = (site * 205) >> 11
    patch = (line >> 1) * 5 + ((site - line * 10) >> 1)
    row_patch = lax.broadcasted_iota(jnp.int32, (ROWS, 128), 0) >> 3
    own_spins = jnp.concatenate([spin_pad[...]] * PATCHES, axis=0)
    picked = jnp.where(patch == row_patch, own_spins, 0.0)
    offsets = jnp.concatenate(
        [jnp.broadcast_to(table[8 + p : 9 + p, :], (OWN, 128)) for p in range(PATCHES)], axis=0
    )
    hidden = (jnp.dot(picked, spread, precision=HI, preferred_element_type=F32) + offsets).astype(BF16)
    w_pad[...] = jnp.zeros_like(w_pad)
    w_pad[:, 0:D] = w_ref[...].astype(F32)
    act = lax.dot_general(
        hidden, w_pad[...].astype(BF16), (((1,), (1,)), ((), ())), preferred_element_type=F32
    ) + bias_ref[...]
    slope_pad[...] = jnp.zeros_like(slope_pad)
    slope_pad[0:ROWS, 0:FOWN] = readout_ref[...] * jnp.tanh(act)
    slope_t = jnp.transpose(slope_pad[...])[0:FOWN, :]
    sample = lax.broadcasted_iota(jnp.int32, (OWN, 256), 0)
    row_sample = lax.broadcasted_iota(jnp.int32, (OWN, 256), 1) & 7
    same = (sample == row_sample)[None]
    left = jnp.where(same, jnp.broadcast_to(slope_t[:, None, :], (FOWN, OWN, 256)), 0.0)
    left = left.reshape(FOWN * OWN, 256)
    right = jnp.concatenate([hidden.astype(F32), jnp.zeros((256 - ROWS, 128), F32)], axis=0)
    return jnp.dot(left, right, precision=HI, preferred_element_type=F32)


def solve(gram_ref, shift, target, upper_ref, scaled_ref):
    lane = lax.broadcasted_iota(jnp.int32, (8, 128), 1)
    sub = lax.broadcasted_iota(jnp.int32, (8, 128), 0)
    tiles = PANEL // 8
    panels = SAMPLES // PANEL
    reach = {}
    for m in range(panels):
        base = PANEL * m
        diag, off = base // 128, base % 128
        for n in (0, 1) if m == 0 else ((m + 1,) if m + 1 < panels else ()):
            first = PANEL * n
            owed = None
            if m:
                row = lax.broadcasted_iota(jnp.int32, (base, 128), 0)
                col = lax.broadcasted_iota(jnp.int32, (base, 128), 1)
                right = []
                for half in range(2):
                    part = scaled_ref[0:base, 128 * half : 128 * half + 128]
                    if half < diag:
                        part = jnp.where(col + 128 * half <= row, part, 0.0)
                    elif half == diag:
                        part = jnp.where((col >= off) | (col + 128 * half <= row), part, 0.0)
                    right.append(part)
                owed = lax.dot_general(
                    upper_ref[0:base, first : first + PANEL], jnp.concatenate(right, axis=1),
                    (((0,), (0,)), ((), ())), preferred_element_type=F32, precision=HI,
                )
            rows = []
            for tile in range(tiles):
                pair = []
                for half in range(2):
                    part = gram_ref[first // 8 + tile, :, 128 * half : 128 * half + 128]
                    at = first + 8 * tile - 128 * half
                    if 0 <= at < 128:
                        part = jnp.where(lane == sub + at, part + shift, part)
                    if half < diag:
                        part = jnp.zeros_like(part)
                    elif half == diag and off:
                        part = jnp.where(lane >= off, part, 0.0)
                    if owed is not None:
                        part = part - owed[8 * tile : 8 * tile + 8, 128 * half : 128 * half + 128]
                    pair.append(part)
                rows.append(pair)
            reach[n] = rows
        near = [n for n in (m, m + 1) if n < panels]
        inside = (lane >= off) & (lane < off + PANEL)
        column = {}
        for j in range(PANEL):
            for n in near:
                for tile in range(tiles):
                    column[j, n, tile] = jnp.broadcast_to(reach[n][tile][diag][:, off + j : off + j + 1], (8, 128))
        for n in near:
            for tile in range(tiles):
                reach[n][tile][diag] = jnp.where(inside, 0.0, reach[n][tile][diag])
        for j in range(PANEL):
            mine, at = j // 8, j % 8
            inverse = 1.0 / column[j, m, mine][at : at + 1, :]
            live = [
                (n, tile) for n in near for tile in range(tiles)
                if n > m or tile > mine or (tile == mine and at < 7)
            ]
            for k in range(j + 1, PANEL):
                factor = column[k, m, mine][at : at + 1, :] * inverse
                for n, tile in live:
                    column[k, n, tile] = column[k, n, tile] - column[j, n, tile] * factor
            for half in range(2):
                pivot_row = reach[m][mine][half][at : at + 1, :]
                if half == diag:
                    pivot_row = jnp.where(lane[0:1] == off + j, 1.0, pivot_row)
                scaled = pivot_row * inverse
                upper_ref[base + j : base + j + 1, 128 * half : 128 * half + 128] = pivot_row
                scaled_ref[base + j : base + j + 1, 128 * half : 128 * half + 128] = scaled
                for n, tile in live:
                    reach[n][tile][half] = reach[n][tile][half] - column[j, n, tile] * scaled
        del reach[m]
    row = lax.broadcasted_iota(jnp.int32, (SAMPLES, SAMPLES), 0)
    col = lax.broadcasted_iota(jnp.int32, (SAMPLES, SAMPLES), 1)
    low = col <= row
    half_solved = jnp.sum(jnp.where(low, upper_ref[...], 0.0) * target, axis=1, keepdims=True)
    return jnp.sum(jnp.where(low, scaled_ref[...], 0.0) * half_solved, axis=0, keepdims=True)


def kernel(
    spins_hbm, embed_hbm, position_hbm, w_hbm, bias_hbm, readout_hbm, other_hbm, energies_hbm, shift_hbm,
    coeffs_ref, update_ref, rest_ref,
    spins_ref, embed_ref, position_ref, w_ref, bias_ref, readout_ref, other_ref, energies_ref, shift_ref,
    spin_pad, table, w_pad, slope_pad, sbuf, rbuf, cbuf, pair_out, pair_in, half, xy_in, z_in, gram_ref,
    upper, scaled, result, results, send_sem, recv_sem, load_sem,
):
    samp, par, x, zh, y, zl, core = place()
    q = x * 4 + y
    z = zh * 4 + zl
    mate = zl * 2 + (1 - core)

    def samp_peer(k):
        return (lax.rem(samp + k, NSAMP), par)

    def xy_peer(k):
        nx = lax.rem(x + k // 4, 4)
        ny = lax.rem(y + k % 4, 4)
        return nx * 4 + ny, (nx * 8 + zh * 4 + ny, par)

    def z_peer(k):
        nz = lax.rem(z + k, 8)
        return nz, (x * 8 + (nz // 4) * 4 + y, (nz % 4) * 2 + core)

    loads = [
        pltpu.make_async_copy(a, b, load_sem.at[n])
        for n, (a, b) in enumerate(
            (
                (spins_hbm, spins_ref), (embed_hbm, embed_ref), (position_hbm, position_ref), (w_hbm, w_ref),
                (bias_hbm, bias_ref), (readout_hbm, readout_ref), (other_hbm, other_ref),
                (energies_hbm, energies_ref), (shift_hbm, shift_ref),
            )
        )
    ]
    for load in loads:
        load.start()
    barrier = pltpu.get_barrier_semaphore()
    greeted = 0
    for k in range(1, NSAMP):
        pl.semaphore_signal(barrier, inc=1, device_id=samp_peer(k), device_id_type=MESH)
        greeted += 1
    for k in (1, 2, 3, 5, 6, 7):
        pl.semaphore_signal(barrier, inc=1, device_id=z_peer(k)[1], device_id_type=MESH)
        greeted += 1
    pl.semaphore_signal(barrier, inc=1, device_id=(samp, mate), device_id_type=MESH)
    greeted += 1

    for load in loads:
        load.wait()
    grads = local_derivatives(
        spins_ref, embed_ref, position_ref, w_ref, bias_ref, readout_ref, spin_pad, table, w_pad, slope_pad
    )
    lane = lax.broadcasted_iota(jnp.int32, (256, 128), 1)
    high = grads.astype(BF16).astype(F32)
    terms = jnp.where(lane < D, high, grads - high)
    for j in range(NSAMP):
        sbuf[j] = jnp.concatenate(
            [other_ref[:, 128 * j : 128 * (j + 1)].astype(F32), terms[8 * j : 8 * (j + 1), :]], axis=0
        ).astype(BF16)

    pl.semaphore_wait(barrier, greeted)

    for k in range(1, NSAMP):
        to = samp_peer(k)
        pltpu.make_async_remote_copy(
            src_ref=sbuf.at[to[0]], dst_ref=rbuf.at[samp], send_sem=send_sem.at[0], recv_sem=recv_sem.at[0],
            device_id=to, device_id_type=MESH,
        ).start()
    rbuf[samp] = sbuf[samp]
    most = rbuf.at[pl.ds(0, NSAMP - 1)]
    pltpu.make_async_copy(most, most, recv_sem.at[0]).wait()

    got = rbuf[...].astype(F32)
    others = got[:, 0:8, :].reshape(SAMPLES, 128)
    pair = got[:, 8:16, :].reshape(SAMPLES, 128)
    layer = jnp.where(lane < D, pair + pltpu.roll(pair, D, 1), 0.0)
    for n, joined in enumerate((others, layer)):
        mean = jnp.sum(joined, axis=0, keepdims=True) / SAMPLES
        cbuf[:, 128 * n : 128 * (n + 1)] = ((joined - mean) * 0.0625).astype(BF16)

    def rows_of(c):
        return lax.dot_general(
            cbuf[pl.ds(pl.multiple_of(c * 128, 128), 128), :], cbuf[...], (((1,), (1,)), ((), ())),
            preferred_element_type=F32,
        )

    pair_out[...] = rows_of(1 - core)
    swap = pltpu.make_async_remote_copy(
        src_ref=pair_out, dst_ref=pair_in, send_sem=send_sem.at[1], recv_sem=recv_sem.at[1],
        device_id=(samp, mate), device_id_type=MESH,
    )
    swap.start()
    own = rows_of(core)
    swap.wait_recv()
    half[...] = (own + pair_in[...]).reshape(16, 8, 256)

    for k in range(1, 16):
        nq, to = xy_peer(k)
        pltpu.make_async_remote_copy(
            src_ref=half.at[nq], dst_ref=xy_in.at[q], send_sem=send_sem.at[2], recv_sem=recv_sem.at[2],
            device_id=to, device_id_type=MESH,
        ).start()
    xy_in[q] = half[q]
    most = xy_in.at[pl.ds(0, 15)]
    pltpu.make_async_copy(most, most, recv_sem.at[2]).wait()
    z_in[z] = jnp.sum(xy_in[...], axis=0)

    for k in range(1, 8):
        to = z_peer(k)[1]
        pltpu.make_async_remote_copy(
            src_ref=z_in.at[z], dst_ref=z_in.at[z], send_sem=send_sem.at[3], recv_sem=recv_sem.at[3],
            device_id=to, device_id_type=MESH,
        ).start()
    most = z_in.at[pl.ds(0, 7)]
    pltpu.make_async_copy(most, most, recv_sem.at[3]).wait()
    mine = core * 16 + q
    gram_ref[mine] = jnp.sum(z_in[...], axis=0)

    for k in range(1, 16):
        to = xy_peer(k)[1]
        pltpu.make_async_remote_copy(
            src_ref=gram_ref.at[mine], dst_ref=gram_ref.at[mine], send_sem=send_sem.at[4], recv_sem=recv_sem.at[4],
            device_id=to, device_id_type=MESH,
        ).start()
    most = gram_ref.at[pl.ds(core * 16, 15)]
    pltpu.make_async_copy(most, most, recv_sem.at[4]).wait()
    own_half = gram_ref.at[pl.ds(core * 16, 16)]
    swap = pltpu.make_async_remote_copy(
        src_ref=own_half, dst_ref=own_half, send_sem=send_sem.at[5], recv_sem=recv_sem.at[5],
        device_id=(samp, mate), device_id_type=MESH,
    )
    swap.start()
    swap.wait_recv()

    energies = energies_ref[...]
    target = energies - jnp.sum(energies, axis=1, keepdims=True) / SAMPLES
    x = solve(gram_ref, shift_ref[...], target, upper, scaled)
    coeffs_ref[...] = pltpu.roll(
        jnp.broadcast_to(x, (8, SAMPLES)), lax.rem(SAMPLES - OWN * samp, SAMPLES), 1
    )[0:1, 0:OWN]

    first = x.astype(BF16).astype(F32)
    second = (x - first).astype(BF16).astype(F32)
    terms = jnp.concatenate([first, second, x - first - second, jnp.zeros((13, SAMPLES), F32)], axis=0).astype(BF16)
    full = jnp.dot(terms, cbuf[...], preferred_element_type=F32)
    full = full[0:1] + (full[1:2] + full[2:3])
    result[0:1, :] = full[:, 0:128]
    result[1:2, :] = full[:, 128:256]
    for k in range(1, NSAMP):
        pltpu.make_async_remote_copy(
            src_ref=result, dst_ref=results.at[samp], send_sem=send_sem.at[6], recv_sem=recv_sem.at[6],
            device_id=samp_peer(k), device_id_type=MESH,
        ).start()
    results[samp] = result[...]
    most = results.at[pl.ds(0, NSAMP - 1)]
    pltpu.make_async_copy(most, most, recv_sem.at[6]).wait()
    got = results[...]
    rest_ref[...] = got[:, 0, :]
    update_ref[...] = got[:, 1, 0:D]

    for ref, n, size in ((results, 6, 31), (sbuf, 0, 31), (pair_out, 1, None), (half, 2, 15), (z_in, 3, 7), (gram_ref, 4, 15), (gram_ref, 5, 16)):
        part = ref if size is None else ref.at[pl.ds(0, size)]
        pltpu.make_async_copy(part, part, send_sem.at[n]).wait()


def per_device(spins, embed, position, w_first, bias_first, readout, other_grads, energies, shift):
    vmem = pl.BlockSpec(memory_space=pltpu.VMEM)
    operands = (
        spins, embed, position, w_first.T, bias_first.reshape(1, -1), readout.reshape(1, -1), other_grads,
        energies.reshape(1, -1), shift.reshape(1, 1),
    )
    coeffs, update, rest = pl.pallas_call(
        kernel,
        out_shape=(
            jax.ShapeDtypeStruct((1, OWN), F32),
            jax.ShapeDtypeStruct((FOWN, D), F32),
            jax.ShapeDtypeStruct((NSAMP, 128), F32),
        ),
        in_specs=[pl.BlockSpec(memory_space=pltpu.HBM)] * 9,
        out_specs=(vmem,) * 3,
        scratch_shapes=[pltpu.VMEM(a.shape, a.dtype) for a in operands]
        + [
            pltpu.VMEM((8, 128), F32),
            pltpu.VMEM((40, 128), F32),
            pltpu.VMEM((FOWN, 128), F32),
            pltpu.VMEM((256, 128), F32),
            pltpu.VMEM((NSAMP, 16, 128), BF16),
            pltpu.VMEM((NSAMP, 16, 128), BF16),
            pltpu.VMEM((256, 256), BF16),
            pltpu.VMEM((128, 256), F32),
            pltpu.VMEM((128, 256), F32),
            pltpu.VMEM((16, 8, 256), F32),
            pltpu.VMEM((16, 8, 256), F32),
            pltpu.VMEM((8, 8, 256), F32),
            pltpu.VMEM((32, 8, 256), F32),
            pltpu.VMEM((256, 256), F32),
            pltpu.VMEM((256, 256), F32),
            pltpu.VMEM((2, 128), F32),
            pltpu.VMEM((NSAMP, 2, 128), F32),
            pltpu.SemaphoreType.DMA((7,)),
            pltpu.SemaphoreType.DMA((7,)),
            pltpu.SemaphoreType.DMA((9,)),
        ],
        compiler_params=pltpu.CompilerParams(
            collective_id=0, has_side_effects=True, vmem_limit_bytes=32 * 2**20
        ),
        name="update",
    )(*operands)
    return (coeffs.reshape(-1), update.T, rest.reshape(-1))


def solution(mesh):
    return jax.shard_map(
        per_device,
        mesh=mesh,
        in_specs=(
            P("samp", None), P(), P(), P(None, "par"), P("par"), P("par"), P("samp", "par"), P(), P(),
        ),
        out_specs=(P("samp"), P(None, "par"), P("par")),
        check_vma=False,
    )
```

```python
import itertools

import jax
import jax.numpy as jnp
from jax import lax
from jax.experimental import pallas as pl
from jax.experimental.pallas import tpu as pltpu
from jax.sharding import PartitionSpec as P

MESH = pl.DeviceIdType.MESH
HI = lax.Precision.HIGHEST
F32 = jnp.float32
BF16 = jnp.bfloat16

LSIDE = 10
PATCHES = 25
D = 64
SAMPLES = 256
OWN = 8
FOWN = 32
NSAMP = 32
NPAR = 8
NX, NZH, NY = 4, 2, 4
PANEL = 16
ROWS = PATCHES * OWN


def place():
    samp = lax.axis_index("samp")
    par = lax.axis_index("par")
    x, zh, y = samp // 8, (samp // 4) % 2, samp % 4
    zl, core = par // 2, par % 2
    return samp, par, x, zh, y, zl, core


def local_derivatives(spins_ref, embed_ref, position_ref, w_ref, bias_ref, readout_ref, spin_pad, table, w_pad, slope_pad):
    spin_pad[...] = jnp.zeros_like(spin_pad)
    spin_pad[:, 0:100] = spins_ref[...].astype(F32)
    table[0:4, 0:D] = embed_ref[...]
    table[0:4, D : 2 * D] = embed_ref[...]
    table[8 : 8 + PATCHES, 0:D] = position_ref[...]
    table[8 : 8 + PATCHES, D : 2 * D] = position_ref[...]
    site = lax.broadcasted_iota(jnp.int32, (128, 128), 0)
    line = (site * 205) >> 11
    kind = (line & 1) * 2 + ((site - line * 10) & 1)
    spread = jnp.where(
        kind == 0,
        table[0:1, :],
        jnp.where(kind == 1, table[1:2, :], jnp.where(kind == 2, table[2:3, :], table[3:4, :])),
    )
    site = lax.broadcasted_iota(jnp.int32, (ROWS, 128), 1)
    line = (site * 205) >> 11
    patch = (line >> 1) * 5 + ((site - line * 10) >> 1)
    row_patch = lax.broadcasted_iota(jnp.int32, (ROWS, 128), 0) >> 3
    own_spins = jnp.concatenate([spin_pad[...]] * PATCHES, axis=0)
    picked = jnp.where(patch == row_patch, own_spins, 0.0)
    offsets = jnp.concatenate(
        [jnp.broadcast_to(table[8 + p : 9 + p, :], (OWN, 128)) for p in range(PATCHES)], axis=0
    )
    hidden = (jnp.dot(picked, spread, precision=HI, preferred_element_type=F32) + offsets).astype(BF16)
    w_pad[...] = jnp.zeros_like(w_pad)
    w_pad[:, 0:D] = w_ref[...].astype(F32)
    act = lax.dot_general(
        hidden, w_pad[...].astype(BF16), (((1,), (1,)), ((), ())), preferred_element_type=F32
    ) + bias_ref[...]
    slope_pad[...] = jnp.zeros_like(slope_pad)
    slope_pad[0:ROWS, 0:FOWN] = readout_ref[...] * jnp.tanh(act)
    slope_t = jnp.transpose(slope_pad[...])[0:FOWN, :]
    sample = lax.broadcasted_iota(jnp.int32, (OWN, 256), 0)
    row_sample = lax.broadcasted_iota(jnp.int32, (OWN, 256), 1) & 7
    same = (sample == row_sample)[None]
    left = jnp.where(same, jnp.broadcast_to(slope_t[:, None, :], (FOWN, OWN, 256)), 0.0)
    left = left.reshape(FOWN * OWN, 256)
    right = jnp.concatenate([hidden.astype(F32), jnp.zeros((256 - ROWS, 128), F32)], axis=0)
    return jnp.dot(left, right, precision=HI, preferred_element_type=F32)


def gram_tile(gram_ref, row, half):
    return gram_ref[(row // 8) % 2, (row % 8) * 2 + half, row // 16]


def offsets(dims):
    def far(step):
        return sum(4 * d if name == "zh" else min(d, 4 - d) for name, d in zip(dims, step))
    sizes = [2 if name == "zh" else 4 for name in dims]
    return sorted(itertools.product(*map(range, sizes)), key=far, reverse=True)[:-1]


def solve(gram_ref, shift, target, upper_ref, scaled_ref):
    lane = lax.broadcasted_iota(jnp.int32, (8, 128), 1)
    sub = lax.broadcasted_iota(jnp.int32, (8, 128), 0)
    tiles = PANEL // 8
    panels = SAMPLES // PANEL
    reach = {}
    for m in range(panels):
        base = PANEL * m
        diag, off = base // 128, base % 128
        for n in (0, 1) if m == 0 else ((m + 1,) if m + 1 < panels else ()):
            first = PANEL * n
            owed = None
            if m:
                row = lax.broadcasted_iota(jnp.int32, (base, 128), 0)
                col = lax.broadcasted_iota(jnp.int32, (base, 128), 1)
                right = []
                for half in range(2):
                    part = scaled_ref[0:base, 128 * half : 128 * half + 128]
                    if half < diag:
                        part = jnp.where(col + 128 * half <= row, part, 0.0)
                    elif half == diag:
                        part = jnp.where((col >= off) | (col + 128 * half <= row), part, 0.0)
                    right.append(part)
                owed = lax.dot_general(
                    upper_ref[0:base, first : first + PANEL], jnp.concatenate(right, axis=1),
                    (((0,), (0,)), ((), ())), preferred_element_type=F32, precision=HI,
                )
            rows = []
            for tile in range(tiles):
                pair = []
                for half in range(2):
                    part = gram_tile(gram_ref, first // 8 + tile, half)
                    at = first + 8 * tile - 128 * half
                    if 0 <= at < 128:
                        part = jnp.where(lane == sub + at, part + shift, part)
                    if half < diag:
                        part = jnp.zeros_like(part)
                    elif half == diag and off:
                        part = jnp.where(lane >= off, part, 0.0)
                    if owed is not None:
                        part = part - owed[8 * tile : 8 * tile + 8, 128 * half : 128 * half + 128]
                    pair.append(part)
                rows.append(pair)
            reach[n] = rows
        near = [n for n in (m, m + 1) if n < panels]
        inside = (lane >= off) & (lane < off + PANEL)
        column = {}
        for j in range(PANEL):
            for n in near:
                for tile in range(tiles):
                    column[j, n, tile] = jnp.broadcast_to(reach[n][tile][diag][:, off + j : off + j + 1], (8, 128))
        for n in near:
            for tile in range(tiles):
                reach[n][tile][diag] = jnp.where(inside, 0.0, reach[n][tile][diag])
        for j in range(PANEL):
            mine, at = j // 8, j % 8
            inverse = 1.0 / column[j, m, mine][at : at + 1, :]
            live = [
                (n, tile) for n in near for tile in range(tiles)
                if n > m or tile > mine or (tile == mine and at < 7)
            ]
            for k in range(j + 1, PANEL):
                factor = column[k, m, mine][at : at + 1, :] * inverse
                for n, tile in live:
                    column[k, n, tile] = column[k, n, tile] - column[j, n, tile] * factor
            for half in range(2):
                pivot_row = reach[m][mine][half][at : at + 1, :]
                if half == diag:
                    pivot_row = jnp.where(lane[0:1] == off + j, 1.0, pivot_row)
                scaled = pivot_row * inverse
                upper_ref[base + j : base + j + 1, 128 * half : 128 * half + 128] = pivot_row
                scaled_ref[base + j : base + j + 1, 128 * half : 128 * half + 128] = scaled
                for n, tile in live:
                    reach[n][tile][half] = reach[n][tile][half] - column[j, n, tile] * scaled
        del reach[m]
    row = lax.broadcasted_iota(jnp.int32, (SAMPLES, SAMPLES), 0)
    col = lax.broadcasted_iota(jnp.int32, (SAMPLES, SAMPLES), 1)
    low = col <= row
    half_solved = jnp.sum(jnp.where(low, upper_ref[...], 0.0) * target, axis=1, keepdims=True)
    return jnp.sum(jnp.where(low, scaled_ref[...], 0.0) * half_solved, axis=0, keepdims=True)


def kernel(
    spins_hbm, embed_hbm, position_hbm, w_hbm, bias_hbm, readout_hbm, other_hbm, energies_hbm, shift_hbm,
    coeffs_ref, update_ref, rest_ref,
    spins_ref, embed_ref, position_ref, w_ref, bias_ref, readout_ref, other_ref, energies_ref, shift_ref,
    spin_pad, table, w_pad, slope_pad, sbuf, rbuf, cbuf, pair_out, pair_in, half, xy_in, z_in, gram_ref,
    upper, scaled, result, results, send_sem, recv_sem, load_sem,
):
    samp, par, x, zh, y, zl, core = place()
    q = x * 4 + y
    z = zh * 4 + zl
    mate = (samp, zl * 2 + (1 - core))

    def samp_peer(step):
        dx, dz, dy = step
        nq = lax.rem(x + dx, 4) * 4 + lax.rem(y + dy, 4)
        return nq, ((nq // 4) * 8 + lax.rem(zh + dz, 2) * 4 + nq % 4, par)

    def xy_peer(step):
        return samp_peer((step[0], 0, step[1]))

    def z_peer(k):
        nz = lax.rem(z + k, 8)
        return (x * 8 + (nz // 4) * 4 + y, (nz % 4) * 2 + core)

    plane = offsets(("x", "y"))
    group = offsets(("x", "zh", "y"))
    column = (4, 3, 5, 2, 6, 1, 7)

    barrier = pltpu.get_barrier_semaphore()
    greet = [samp_peer(step)[1] for step in group] + [z_peer(k) for k in column if k != 4] + [mate]
    for to in greet:
        pl.semaphore_signal(barrier, inc=1, device_id=to, device_id_type=MESH)
    loads = [
        pltpu.make_async_copy(a, b, load_sem.at[n])
        for n, (a, b) in enumerate(
            (
                (spins_hbm, spins_ref), (embed_hbm, embed_ref), (position_hbm, position_ref), (w_hbm, w_ref),
                (bias_hbm, bias_ref), (readout_hbm, readout_ref), (other_hbm, other_ref),
                (energies_hbm, energies_ref), (shift_hbm, shift_ref),
            )
        )
    ]
    for load in loads:
        load.start()
    for load in loads:
        load.wait()

    grads = local_derivatives(
        spins_ref, embed_ref, position_ref, w_ref, bias_ref, readout_ref, spin_pad, table, w_pad, slope_pad
    ).reshape(16, 2, OWN, 128)
    lane = lax.broadcasted_iota(jnp.int32, (16, OWN, 128), 2)
    own = jnp.where(lane < D, grads[:, 0], grads[:, 1])
    high = own.astype(BF16).astype(F32)
    low = own - high
    for n in range(16):
        sbuf[n] = jnp.concatenate(
            [
                other_ref[:, 256 * n : 256 * n + 128].astype(F32),
                other_ref[:, 256 * n + 128 : 256 * n + 256].astype(F32),
                high[n],
                low[n],
            ],
            axis=0,
        ).astype(BF16)

    pl.semaphore_wait(barrier, len(greet))

    for step in group:
        nq, to = samp_peer(step)
        pltpu.make_async_remote_copy(
            src_ref=sbuf.at[nq], dst_ref=rbuf.at[samp], send_sem=send_sem.at[0], recv_sem=recv_sem.at[0],
            device_id=to, device_id_type=MESH,
        ).start()
    rbuf[samp] = sbuf[q]
    most = rbuf.at[pl.ds(0, NSAMP - 1)]
    pltpu.make_async_copy(most, most, recv_sem.at[0]).wait()

    got = rbuf[...].astype(F32)
    parts = [got[:, 8 * n : 8 * n + 8, :].reshape(SAMPLES, 128) for n in range(4)]
    for n, joined in enumerate((parts[0], parts[1], parts[2] + parts[3])):
        mean = jnp.sum(joined, axis=0, keepdims=True) / SAMPLES
        cbuf[:, 128 * n : 128 * (n + 1)] = ((joined - mean) * 0.0625).astype(BF16)

    def rows_of(c):
        first = pl.multiple_of(zh * 128 + c * 64, 64)
        return lax.dot_general(
            cbuf[pl.ds(first, 64), :], cbuf[...], (((1,), (1,)), ((), ())), preferred_element_type=F32
        )

    theirs = rows_of(1 - core)
    for n in range(16):
        pair_out[n] = theirs[8 * (n // 2) : 8 * (n // 2) + 8, 128 * (n % 2) : 128 * (n % 2) + 128]
    swap = pltpu.make_async_remote_copy(
        src_ref=pair_out, dst_ref=pair_in, send_sem=send_sem.at[1], recv_sem=recv_sem.at[1],
        device_id=mate, device_id_type=MESH,
    )
    swap.start()
    ours = rows_of(core)
    for n in range(16):
        half[n] = ours[8 * (n // 2) : 8 * (n // 2) + 8, 128 * (n % 2) : 128 * (n % 2) + 128]
    swap.wait_recv()
    half[...] += pair_in[...]

    for step in plane:
        nq, to = xy_peer(step)
        pltpu.make_async_remote_copy(
            src_ref=half.at[nq], dst_ref=xy_in.at[q], send_sem=send_sem.at[2], recv_sem=recv_sem.at[2],
            device_id=to, device_id_type=MESH,
        ).start()
    xy_in[q] = half[q]
    most = xy_in.at[pl.ds(0, 15)]
    pltpu.make_async_copy(most, most, recv_sem.at[2]).wait()
    z_in[z] = jnp.sum(xy_in[...], axis=0)

    for k in column:
        pltpu.make_async_remote_copy(
            src_ref=z_in.at[z], dst_ref=z_in.at[z], send_sem=send_sem.at[3], recv_sem=recv_sem.at[3],
            device_id=z_peer(k), device_id_type=MESH,
        ).start()
    most = z_in.at[pl.ds(0, 7)]
    pltpu.make_async_copy(most, most, recv_sem.at[3]).wait()
    for n in range(2):
        gram_ref[core, q, n] = jnp.sum(z_in[4 * n : 4 * n + 4], axis=0)

    for step in plane:
        pltpu.make_async_remote_copy(
            src_ref=gram_ref.at[core, q], dst_ref=gram_ref.at[core, q], send_sem=send_sem.at[4],
            recv_sem=recv_sem.at[4], device_id=xy_peer(step)[1], device_id_type=MESH,
        ).start()
    most = gram_ref.at[core, pl.ds(0, 15)]
    pltpu.make_async_copy(most, most, recv_sem.at[4]).wait()
    swap = pltpu.make_async_remote_copy(
        src_ref=gram_ref.at[core], dst_ref=gram_ref.at[core], send_sem=send_sem.at[5], recv_sem=recv_sem.at[5],
        device_id=mate, device_id_type=MESH,
    )
    swap.start()
    swap.wait_recv()

    energies = energies_ref[...]
    target = energies - jnp.sum(energies, axis=1, keepdims=True) / SAMPLES
    x_row = solve(gram_ref, shift_ref[...], target, upper, scaled)
    coeffs_ref[...] = pltpu.roll(
        jnp.broadcast_to(x_row, (8, SAMPLES)), lax.rem(SAMPLES - OWN * samp, SAMPLES), 1
    )[0:1, 0:OWN]

    first = x_row.astype(BF16).astype(F32)
    second = (x_row - first).astype(BF16).astype(F32)
    terms = jnp.concatenate([first, second, x_row - first - second, jnp.zeros((13, SAMPLES), F32)], axis=0).astype(BF16)
    full = jnp.dot(terms, cbuf[...], preferred_element_type=F32)
    full = full[0:1] + (full[1:2] + full[2:3])
    for n in range(3):
        result[n : n + 1, :] = full[:, 128 * n : 128 * n + 128]
    result[3:4, :] = full[:, 0:128]
    for step in plane:
        pltpu.make_async_remote_copy(
            src_ref=result, dst_ref=results.at[q], send_sem=send_sem.at[6], recv_sem=recv_sem.at[6],
            device_id=xy_peer(step)[1], device_id_type=MESH,
        ).start()
    results[q] = result[...]
    most = results.at[pl.ds(0, 15)]
    pltpu.make_async_copy(most, most, recv_sem.at[6]).wait()
    rest_ref[...] = results[:, 0:2, :]
    update_ref[...] = results[:, 2, :]

    for part, n in (
        (rbuf.at[pl.ds(0, 31)], 0), (pair_out, 1), (half.at[pl.ds(0, 15)], 2), (z_in.at[pl.ds(0, 7)], 3),
        (gram_ref.at[0, pl.ds(0, 15)], 4), (gram_ref.at[0], 5), (results.at[pl.ds(0, 15)], 6),
    ):
        pltpu.make_async_copy(part, part, send_sem.at[n]).wait()


def per_device(spins, embed, position, w_first, bias_first, readout, other_grads, energies, shift):
    vmem = pl.BlockSpec(memory_space=pltpu.VMEM)
    operands = (
        spins, embed, position, w_first.T, bias_first.reshape(1, -1), readout.reshape(1, -1), other_grads,
        energies.reshape(1, -1), shift.reshape(1, 1),
    )
    operands = tuple(pltpu.with_memory_space_constraint(a, pltpu.HBM) for a in operands[:-1]) + operands[-1:]
    coeffs, update, rest = pl.pallas_call(
        kernel,
        out_shape=(
            jax.ShapeDtypeStruct((1, OWN), F32),
            jax.ShapeDtypeStruct((16, 128), F32),
            jax.ShapeDtypeStruct((16, 2, 128), F32),
        ),
        in_specs=[pl.BlockSpec(memory_space=pltpu.HBM)] * 9,
        out_specs=(vmem,) * 3,
        scratch_shapes=[pltpu.VMEM(a.shape, a.dtype) for a in operands]
        + [
            pltpu.VMEM((8, 128), F32),
            pltpu.VMEM((40, 128), F32),
            pltpu.VMEM((FOWN, 128), F32),
            pltpu.VMEM((256, 128), F32),
            pltpu.VMEM((16, 32, 128), BF16),
            pltpu.VMEM((NSAMP, 32, 128), BF16),
            pltpu.VMEM((SAMPLES, 384), BF16),
            pltpu.VMEM((16, 8, 128), F32),
            pltpu.VMEM((16, 8, 128), F32),
            pltpu.VMEM((16, 8, 128), F32),
            pltpu.VMEM((16, 8, 128), F32),
            pltpu.VMEM((8, 8, 128), F32),
            pltpu.VMEM((2, 16, 2, 8, 128), F32),
            pltpu.VMEM((SAMPLES, SAMPLES), F32),
            pltpu.VMEM((SAMPLES, SAMPLES), F32),
            pltpu.VMEM((4, 128), F32),
            pltpu.VMEM((16, 4, 128), F32),
            pltpu.SemaphoreType.DMA((7,)),
            pltpu.SemaphoreType.DMA((7,)),
            pltpu.SemaphoreType.DMA((9,)),
        ],
        compiler_params=pltpu.CompilerParams(
            collective_id=0, has_side_effects=True, vmem_limit_bytes=32 * 2**20
        ),
        name="update",
    )(*operands)
    return (coeffs.reshape(-1), update.reshape(FOWN, D).T, rest.reshape(-1))


def solution(mesh):
    return jax.shard_map(
        per_device,
        mesh=mesh,
        in_specs=(
            P("samp", None), P(), P(), P(None, "par"), P("par"), P("par"), P("samp", "par"), P(), P(),
        ),
        out_specs=(P("samp"), P(None, "par"), P("par")),
        check_vma=False,
    )
```

```python
import itertools

import jax
import jax.numpy as jnp
from jax import lax
from jax.experimental import pallas as pl
from jax.experimental.pallas import tpu as pltpu
from jax.sharding import PartitionSpec as P

MESH = pl.DeviceIdType.MESH
HI = lax.Precision.HIGHEST
F32 = jnp.float32
BF16 = jnp.bfloat16

LSIDE = 10
PATCHES = 25
D = 64
SAMPLES = 256
OWN = 8
FOWN = 32
NSAMP = 32
NPAR = 8
NX, NZH, NY = 4, 2, 4
PANEL = 16
ROWS = PATCHES * OWN


def place():
    samp = lax.axis_index("samp")
    par = lax.axis_index("par")
    x, zh, y = samp // 8, (samp // 4) % 2, samp % 4
    zl, core = par // 2, par % 2
    return samp, par, x, zh, y, zl, core


def local_derivatives(spins_ref, embed_ref, position_ref, w_ref, bias_ref, readout_ref, spin_pad, table, w_pad, slope_pad):
    spin_pad[...] = jnp.zeros_like(spin_pad)
    spin_pad[:, 0:100] = spins_ref[...].astype(F32)
    table[0:4, 0:D] = embed_ref[...]
    table[0:4, D : 2 * D] = embed_ref[...]
    table[8 : 8 + PATCHES, 0:D] = position_ref[...]
    table[8 : 8 + PATCHES, D : 2 * D] = position_ref[...]
    site = lax.broadcasted_iota(jnp.int32, (128, 128), 0)
    line = (site * 205) >> 11
    kind = (line & 1) * 2 + ((site - line * 10) & 1)
    spread = jnp.where(
        kind == 0,
        table[0:1, :],
        jnp.where(kind == 1, table[1:2, :], jnp.where(kind == 2, table[2:3, :], table[3:4, :])),
    )
    site = lax.broadcasted_iota(jnp.int32, (ROWS, 128), 1)
    line = (site * 205) >> 11
    patch = (line >> 1) * 5 + ((site - line * 10) >> 1)
    row_patch = lax.broadcasted_iota(jnp.int32, (ROWS, 128), 0) >> 3
    own_spins = jnp.concatenate([spin_pad[...]] * PATCHES, axis=0)
    picked = jnp.where(patch == row_patch, own_spins, 0.0)
    offsets = jnp.concatenate(
        [jnp.broadcast_to(table[8 + p : 9 + p, :], (OWN, 128)) for p in range(PATCHES)], axis=0
    )
    hidden = (jnp.dot(picked, spread, precision=HI, preferred_element_type=F32) + offsets).astype(BF16)
    w_pad[...] = jnp.zeros_like(w_pad)
    w_pad[:, 0:D] = w_ref[...].astype(F32)
    act = lax.dot_general(
        hidden, w_pad[...].astype(BF16), (((1,), (1,)), ((), ())), preferred_element_type=F32
    ) + bias_ref[...]
    slope_pad[...] = jnp.zeros_like(slope_pad)
    slope_pad[0:ROWS, 0:FOWN] = readout_ref[...] * jnp.tanh(act)
    slope_t = jnp.transpose(slope_pad[...])[0:FOWN, :]
    sample = lax.broadcasted_iota(jnp.int32, (OWN, 256), 0)
    row_sample = lax.broadcasted_iota(jnp.int32, (OWN, 256), 1) & 7
    same = (sample == row_sample)[None]
    left = jnp.where(same, jnp.broadcast_to(slope_t[:, None, :], (FOWN, OWN, 256)), 0.0)
    left = left.reshape(FOWN * OWN, 256)
    right = jnp.concatenate([hidden.astype(F32), jnp.zeros((256 - ROWS, 128), F32)], axis=0)
    return jnp.dot(left, right, precision=HI, preferred_element_type=F32)


def offsets(dims):
    def far(step):
        return sum({"zh": 4 * d, "core": 0}.get(name, min(d, 4 - d)) for name, d in zip(dims, step))
    sizes = [4 if name in "xy" else 2 for name in dims]
    return sorted(filter(any, itertools.product(*map(range, sizes))), key=far, reverse=True)


def solve(gram_ref, shift, target, upper_ref, scaled_ref):
    lane = lax.broadcasted_iota(jnp.int32, (8, 128), 1)
    sub = lax.broadcasted_iota(jnp.int32, (8, 128), 0)
    tiles = PANEL // 8
    panels = SAMPLES // PANEL
    reach = {}
    for m in range(panels):
        base = PANEL * m
        diag, off = base // 128, base % 128
        for n in (0, 1) if m == 0 else ((m + 1,) if m + 1 < panels else ()):
            first = PANEL * n
            owed = None
            if m:
                row = lax.broadcasted_iota(jnp.int32, (base, 128), 0)
                col = lax.broadcasted_iota(jnp.int32, (base, 128), 1)
                right = []
                for half in range(2):
                    part = scaled_ref[0:base, 128 * half : 128 * half + 128]
                    if half < diag:
                        part = jnp.where(col + 128 * half <= row, part, 0.0)
                    elif half == diag:
                        part = jnp.where((col >= off) | (col + 128 * half <= row), part, 0.0)
                    right.append(part)
                owed = lax.dot_general(
                    upper_ref[0:base, first : first + PANEL], jnp.concatenate(right, axis=1),
                    (((0,), (0,)), ((), ())), preferred_element_type=F32, precision=HI,
                )
            rows = []
            for tile in range(tiles):
                pair = []
                for half in range(2):
                    part = gram_ref[first // 8 + tile, :, 128 * half : 128 * half + 128]
                    at = first + 8 * tile - 128 * half
                    if 0 <= at < 128:
                        part = jnp.where(lane == sub + at, part + shift, part)
                    if half < diag:
                        part = jnp.zeros_like(part)
                    elif half == diag and off:
                        part = jnp.where(lane >= off, part, 0.0)
                    if owed is not None:
                        part = part - owed[8 * tile : 8 * tile + 8, 128 * half : 128 * half + 128]
                    pair.append(part)
                rows.append(pair)
            reach[n] = rows
        near = [n for n in (m, m + 1) if n < panels]
        inside = (lane >= off) & (lane < off + PANEL)
        column = {}
        for j in range(PANEL):
            for n in near:
                for tile in range(tiles):
                    column[j, n, tile] = jnp.broadcast_to(reach[n][tile][diag][:, off + j : off + j + 1], (8, 128))
        for n in near:
            for tile in range(tiles):
                reach[n][tile][diag] = jnp.where(inside, 0.0, reach[n][tile][diag])
        for j in range(PANEL):
            mine, at = j // 8, j % 8
            inverse = 1.0 / column[j, m, mine][at : at + 1, :]
            live = [
                (n, tile) for n in near for tile in range(tiles)
                if n > m or tile > mine or (tile == mine and at < 7)
            ]
            for k in range(j + 1, PANEL):
                factor = column[k, m, mine][at : at + 1, :] * inverse
                for n, tile in live:
                    column[k, n, tile] = column[k, n, tile] - column[j, n, tile] * factor
            for half in range(2):
                pivot_row = reach[m][mine][half][at : at + 1, :]
                if half == diag:
                    pivot_row = jnp.where(lane[0:1] == off + j, 1.0, pivot_row)
                scaled = pivot_row * inverse
                upper_ref[base + j : base + j + 1, 128 * half : 128 * half + 128] = pivot_row
                scaled_ref[base + j : base + j + 1, 128 * half : 128 * half + 128] = scaled
                for n, tile in live:
                    reach[n][tile][half] = reach[n][tile][half] - column[j, n, tile] * scaled
        del reach[m]
    row = lax.broadcasted_iota(jnp.int32, (SAMPLES, SAMPLES), 0)
    col = lax.broadcasted_iota(jnp.int32, (SAMPLES, SAMPLES), 1)
    low = col <= row
    half_solved = jnp.sum(jnp.where(low, upper_ref[...], 0.0) * target, axis=1, keepdims=True)
    return jnp.sum(jnp.where(low, scaled_ref[...], 0.0) * half_solved, axis=0, keepdims=True)


def kernel(
    spins_hbm, embed_hbm, position_hbm, w_hbm, bias_hbm, readout_hbm, other_hbm, energies_hbm, shift_hbm,
    coeffs_ref, update_ref, rest_ref,
    spins_ref, embed_ref, position_ref, w_ref, bias_ref, readout_ref, other_ref, energies_ref, shift_ref,
    spin_pad, table, w_pad, slope_pad, sbuf, rbuf, cbuf, gram_part, plane_in, z_in, gram_ref,
    upper, scaled, result, results, send_sem, recv_sem, load_sem,
):
    samp, par, x, zh, y, zl, core = place()
    q = x * 4 + y
    z = zh * 4 + zl
    mine = q * 2 + core
    owner = zh == zl // 3

    def samp_peer(step):
        dx, dz, dy = step
        nq = lax.rem(x + dx, 4) * 4 + lax.rem(y + dy, 4)
        return nq, ((nq // 4) * 8 + lax.rem(zh + dz, 2) * 4 + nq % 4, par)

    def plane_peer(step):
        dx, dy, dc = step
        nq, (to, _) = samp_peer((dx, 0, dy))
        nc = lax.rem(core + dc, 2)
        return nq * 2 + nc, (to, zl * 2 + nc)

    def z_peer(k):
        nz = lax.rem(z + k, 8)
        return (x * 8 + (nz // 4) * 4 + y, (nz % 4) * 2 + core)

    group = offsets(("x", "zh", "y"))
    plane = offsets(("x", "y", "core"))
    column = (4, 3, 5, 2, 6, 1, 7)

    barrier = pltpu.get_barrier_semaphore()
    greet = [samp_peer(step)[1] for step in group] + [z_peer(k) for k in column if k != 4]
    greet += [plane_peer(step)[1] for step in plane if step[2]]
    for to in greet:
        pl.semaphore_signal(barrier, inc=1, device_id=to, device_id_type=MESH)
    loads = [
        pltpu.make_async_copy(a, b, load_sem.at[n])
        for n, (a, b) in enumerate(
            (
                (spins_hbm, spins_ref), (embed_hbm, embed_ref), (position_hbm, position_ref), (w_hbm, w_ref),
                (bias_hbm, bias_ref), (readout_hbm, readout_ref), (other_hbm, other_ref),
                (energies_hbm, energies_ref), (shift_hbm, shift_ref),
            )
        )
    ]
    for load in loads:
        load.start()
    for load in loads:
        load.wait()

    grads = local_derivatives(
        spins_ref, embed_ref, position_ref, w_ref, bias_ref, readout_ref, spin_pad, table, w_pad, slope_pad
    ).reshape(16, 2, OWN, 128)
    lane = lax.broadcasted_iota(jnp.int32, (16, OWN, 128), 2)
    own = jnp.where(lane < D, grads[:, 0], grads[:, 1])
    high = own.astype(BF16).astype(F32)
    low = own - high
    for n in range(16):
        sbuf[n] = jnp.concatenate(
            [
                other_ref[:, 256 * n : 256 * n + 128].astype(F32),
                other_ref[:, 256 * n + 128 : 256 * n + 256].astype(F32),
                high[n],
                low[n],
            ],
            axis=0,
        ).astype(BF16)

    pl.semaphore_wait(barrier, len(greet))

    for step in group:
        nq, to = samp_peer(step)
        pltpu.make_async_remote_copy(
            src_ref=sbuf.at[nq], dst_ref=rbuf.at[samp], send_sem=send_sem.at[0], recv_sem=recv_sem.at[0],
            device_id=to, device_id_type=MESH,
        ).start()
    rbuf[samp] = sbuf[q]
    most = rbuf.at[pl.ds(0, NSAMP - 1)]
    pltpu.make_async_copy(most, most, recv_sem.at[0]).wait()

    got = rbuf[...].astype(F32)
    parts = [got[:, 8 * n : 8 * n + 8, :].reshape(SAMPLES, 128) for n in range(4)]
    for n, joined in enumerate((parts[0], parts[1], parts[2] + parts[3])):
        mean = jnp.sum(joined, axis=0, keepdims=True) / SAMPLES
        cbuf[:, 128 * n : 128 * (n + 1)] = ((joined - mean) * 0.0625).astype(BF16)

    @pl.when(owner)
    def _():
        gram_part[...] = lax.dot_general(
            cbuf[...], cbuf[...], (((1,), (1,)), ((), ())), preferred_element_type=F32
        ).reshape(32, 8, SAMPLES)
        for step in plane:
            to, device = plane_peer(step)
            pltpu.make_async_remote_copy(
                src_ref=gram_part.at[to], dst_ref=plane_in.at[mine], send_sem=send_sem.at[1], recv_sem=recv_sem.at[1],
                device_id=device, device_id_type=MESH,
            ).start()
        plane_in[mine] = gram_part[mine]
        most = plane_in.at[pl.ds(0, 31)]
        pltpu.make_async_copy(most, most, recv_sem.at[1]).wait()
        z_in[zl] = jnp.sum(plane_in[...], axis=0)

        for k in column:
            pltpu.make_async_remote_copy(
                src_ref=z_in.at[zl], dst_ref=z_in.at[zl], send_sem=send_sem.at[2], recv_sem=recv_sem.at[2],
                device_id=z_peer(k), device_id_type=MESH,
            ).start()
        most = z_in.at[pl.ds(0, 3)]
        pltpu.make_async_copy(most, most, recv_sem.at[2]).wait()

    @pl.when(jnp.logical_not(owner))
    def _():
        pltpu.make_async_copy(z_in, z_in, recv_sem.at[2]).wait()

    gram_ref[mine] = jnp.sum(z_in[...], axis=0)

    for step in plane:
        pltpu.make_async_remote_copy(
            src_ref=gram_ref.at[mine], dst_ref=gram_ref.at[mine], send_sem=send_sem.at[3],
            recv_sem=recv_sem.at[3], device_id=plane_peer(step)[1], device_id_type=MESH,
        ).start()
    most = gram_ref.at[pl.ds(0, 31)]
    pltpu.make_async_copy(most, most, recv_sem.at[3]).wait()

    energies = energies_ref[...]
    target = energies - jnp.sum(energies, axis=1, keepdims=True) / SAMPLES
    x_row = solve(gram_ref, shift_ref[...], target, upper, scaled)
    coeffs_ref[...] = pltpu.roll(
        jnp.broadcast_to(x_row, (8, SAMPLES)), lax.rem(SAMPLES - OWN * samp, SAMPLES), 1
    )[0:1, 0:OWN]

    first = x_row.astype(BF16).astype(F32)
    second = (x_row - first).astype(BF16).astype(F32)
    terms = jnp.concatenate([first, second, x_row - first - second, jnp.zeros((13, SAMPLES), F32)], axis=0).astype(BF16)
    full = jnp.dot(terms, cbuf[...], preferred_element_type=F32)
    full = full[0:1] + (full[1:2] + full[2:3])
    for n in range(3):
        result[n : n + 1, :] = full[:, 128 * n : 128 * n + 128]
    result[3:4, :] = full[:, 0:128]
    for step in plane:
        if step[2] == 0:
            pltpu.make_async_remote_copy(
                src_ref=result, dst_ref=results.at[q], send_sem=send_sem.at[4], recv_sem=recv_sem.at[4],
                device_id=plane_peer(step)[1], device_id_type=MESH,
            ).start()
    results[q] = result[...]
    most = results.at[pl.ds(0, 15)]
    pltpu.make_async_copy(most, most, recv_sem.at[4]).wait()
    rest_ref[...] = results[:, 0:2, :]
    update_ref[...] = results[:, 2, :]

    @pl.when(owner)
    def _():
        for part, n in ((plane_in.at[pl.ds(0, 31)], 1), (plane_in.at[pl.ds(0, 7)], 2)):
            pltpu.make_async_copy(part, part, send_sem.at[n]).wait()

    for part, n in ((rbuf.at[pl.ds(0, 31)], 0), (gram_ref.at[pl.ds(0, 31)], 3), (results.at[pl.ds(0, 15)], 4)):
        pltpu.make_async_copy(part, part, send_sem.at[n]).wait()


def per_device(spins, embed, position, w_first, bias_first, readout, other_grads, energies, shift):
    vmem = pl.BlockSpec(memory_space=pltpu.VMEM)
    operands = (
        spins, embed, position, w_first.T, bias_first.reshape(1, -1), readout.reshape(1, -1), other_grads,
        energies.reshape(1, -1), shift.reshape(1, 1),
    )
    operands = tuple(pltpu.with_memory_space_constraint(a, pltpu.HBM) for a in operands[:-1]) + operands[-1:]
    coeffs, update, rest = pl.pallas_call(
        kernel,
        out_shape=(
            jax.ShapeDtypeStruct((1, OWN), F32),
            jax.ShapeDtypeStruct((16, 128), F32),
            jax.ShapeDtypeStruct((16, 2, 128), F32),
        ),
        in_specs=[pl.BlockSpec(memory_space=pltpu.HBM)] * 9,
        out_specs=(vmem,) * 3,
        scratch_shapes=[pltpu.VMEM(a.shape, a.dtype) for a in operands]
        + [
            pltpu.VMEM((8, 128), F32),
            pltpu.VMEM((40, 128), F32),
            pltpu.VMEM((FOWN, 128), F32),
            pltpu.VMEM((256, 128), F32),
            pltpu.VMEM((16, 32, 128), BF16),
            pltpu.VMEM((NSAMP, 32, 128), BF16),
            pltpu.VMEM((SAMPLES, 384), BF16),
            pltpu.VMEM((32, 8, SAMPLES), F32),
            pltpu.VMEM((32, 8, SAMPLES), F32),
            pltpu.VMEM((4, 8, SAMPLES), F32),
            pltpu.VMEM((32, 8, SAMPLES), F32),
            pltpu.VMEM((SAMPLES, SAMPLES), F32),
            pltpu.VMEM((SAMPLES, SAMPLES), F32),
            pltpu.VMEM((4, 128), F32),
            pltpu.VMEM((16, 4, 128), F32),
            pltpu.SemaphoreType.DMA((5,)),
            pltpu.SemaphoreType.DMA((5,)),
            pltpu.SemaphoreType.DMA((9,)),
        ],
        compiler_params=pltpu.CompilerParams(
            collective_id=0, has_side_effects=True, vmem_limit_bytes=32 * 2**20
        ),
        name="update",
    )(*operands)
    return (coeffs.reshape(-1), update.reshape(FOWN, D).T, rest.reshape(-1))


def solution(mesh):
    return jax.shard_map(
        per_device,
        mesh=mesh,
        in_specs=(
            P("samp", None), P(), P(), P(None, "par"), P("par"), P("par"), P("samp", "par"), P(), P(),
        ),
        out_specs=(P("samp"), P(None, "par"), P("par")),
        check_vma=False,
    )
```

```python
import functools
import itertools

import jax
import jax.numpy as jnp
from jax import lax
from jax.experimental import pallas as pl
from jax.experimental.pallas import tpu as pltpu
from jax.sharding import PartitionSpec as P

MESH = pl.DeviceIdType.MESH
HI = lax.Precision.HIGHEST
F32 = jnp.float32
BF16 = jnp.bfloat16

LSIDE = 10
PATCHES = 25
D = 64
SAMPLES = 256
OWN = 8
FOWN = 32
NSAMP = 32
NPAR = 8
NX, NZH, NY = 4, 2, 4
PANEL = 16
ROWS = 512


def place():
    samp = lax.axis_index("samp")
    par = lax.axis_index("par")
    x, zh, y = samp // 8, (samp // 4) % 2, samp % 4
    zl, core = par // 2, par % 2
    return samp, par, x, zh, y, zl, core


def site_patch(site):
    line = (site * 205) >> 11
    at = site - line * 10
    return (line >> 1) * 5 + (at >> 1), (line & 1) * 2 + (at & 1)


def patterns(shape, dim):
    pattern = lax.broadcasted_iota(jnp.int32, shape, dim) & 15
    return [jnp.where((pattern >> k) & 1 == 1, 1.0, -1.0) for k in range(4)]


def tables(q, embed_ref, position_ref, w_ref, bias_ref, readout_ref, table, w_pad, terms, match):
    for half in (0, D):
        table[0:4, half : half + D] = embed_ref[...]
        table[8 : 8 + PATCHES, half : half + D] = position_ref[...]
    hidden = sum(sign * table[k : k + 1, :] for k, sign in enumerate(patterns((ROWS, 128), 0)))
    hidden += jnp.concatenate(
        [jnp.broadcast_to(table[8 + p : 9 + p, :], (16, 128)) for p in range(PATCHES)]
        + [jnp.zeros((ROWS - 16 * PATCHES, 128), F32)], axis=0
    )
    hidden = hidden.astype(BF16)
    w_pad[...] = jnp.zeros_like(w_pad)
    w_pad[:, 0:D] = w_ref[...].astype(F32)
    units = jnp.concatenate(
        [jnp.broadcast_to(w_pad[pl.ds(2 * q + n, 1), :], (D, 128)) for n in range(2)], axis=0
    ).astype(BF16)
    lane = lax.broadcasted_iota(jnp.int32, (1, 128), 1)
    unit = lax.broadcasted_iota(jnp.int32, (1, FOWN), 1)

    def along(ref):
        both = [jnp.sum(jnp.where(unit == 2 * q + n, ref[...], 0.0), axis=1, keepdims=True) for n in range(2)]
        return jnp.where(lane < D, both[0], both[1])

    act = lax.dot_general(hidden, units, (((1,), (1,)), ((), ())), preferred_element_type=F32) + along(bias_ref)
    rest = hidden.astype(F32) * (along(readout_ref) * jnp.tanh(act))
    for n in range(3):
        term = rest.astype(BF16)
        terms[:, 128 * n : 128 * n + 128] = term
        rest = rest - term.astype(F32)
    shape = (128, ROWS)
    patch, place_in = site_patch(lax.broadcasted_iota(jnp.int32, shape, 0))
    signs = patterns(shape, 1)
    sign = jnp.where(
        place_in == 0, signs[0], jnp.where(place_in == 1, signs[1], jnp.where(place_in == 2, signs[2], signs[3]))
    )
    match[...] = jnp.where(patch == lax.broadcasted_iota(jnp.int32, shape, 1) >> 4, sign, 0.0).astype(BF16)


def derivatives(spins_all, terms, match):
    got = spins_all[...].astype(F32)
    spins = jnp.concatenate(
        [
            got[x * 4 + y, 8 * zh : 8 * zh + 8, :]
            for x, zh, y in itertools.product(range(NX), range(NZH), range(NY))
        ], axis=0
    ).astype(BF16)
    score = jnp.dot(spins, match[...], preferred_element_type=F32)
    has = jnp.where(score > 3.5, 1.0, 0.0).astype(BF16)
    grads = jnp.dot(has, terms[...], preferred_element_type=F32)
    return grads[:, 0:128] + (grads[:, 128:256] + grads[:, 256:384])


def offsets(dims):
    def far(step):
        return sum({"zh": 4 * d, "core": 0}.get(name, min(d, 4 - d)) for name, d in zip(dims, step))
    sizes = [4 if name in "xy" else 2 for name in dims]
    return sorted(filter(any, itertools.product(*map(range, sizes))), key=far, reverse=True)


def solve(gram_ref, shift, target, upper_ref, scaled_ref):
    lane = lax.broadcasted_iota(jnp.int32, (8, 128), 1)
    sub = lax.broadcasted_iota(jnp.int32, (8, 128), 0)
    tiles = PANEL // 8
    panels = SAMPLES // PANEL
    corner = jnp.transpose(jnp.concatenate([jnp.zeros((112, 128), F32), gram_ref[14, 0], gram_ref[15, 0]], axis=0))
    reach = {}
    for m in range(panels):
        base = PANEL * m
        diag, off = base // 128, base % 128
        for n in (0, 1) if m == 0 else ((m + 1,) if m + 1 < panels else ()):
            first = PANEL * n
            owed = None
            if m:
                row = lax.broadcasted_iota(jnp.int32, (base, 128), 0)
                col = lax.broadcasted_iota(jnp.int32, (base, 128), 1)
                right = []
                for half in range(2):
                    part = scaled_ref[0:base, 128 * half : 128 * half + 128]
                    if half < diag:
                        part = jnp.where(col + 128 * half <= row, part, 0.0)
                    elif half == diag:
                        part = jnp.where((col >= off) | (col + 128 * half <= row), part, 0.0)
                    right.append(part)
                owed = lax.dot_general(
                    upper_ref[0:base, first : first + PANEL], jnp.concatenate(right, axis=1),
                    (((0,), (0,)), ((), ())), preferred_element_type=F32, precision=HI,
                )
            rows = []
            for tile in range(tiles):
                pair = []
                for half in range(2):
                    if half == 0 and first >= 128:
                        part = jnp.zeros((8, 128), F32) if diag else corner[8 * tile : 8 * tile + 8, :]
                    else:
                        part = gram_ref[first // 8 + tile, 1 - half]
                    at = first + 8 * tile - 128 * half
                    if 0 <= at < 128:
                        part = jnp.where(lane == sub + at, part + shift, part)
                    if half < diag:
                        part = jnp.zeros_like(part)
                    elif half == diag and off:
                        part = jnp.where(lane >= off, part, 0.0)
                    if owed is not None:
                        part = part - owed[8 * tile : 8 * tile + 8, 128 * half : 128 * half + 128]
                    pair.append(part)
                rows.append(pair)
            reach[n] = rows
        near = [n for n in (m, m + 1) if n < panels]
        inside = (lane >= off) & (lane < off + PANEL)
        column = {}
        for j in range(PANEL):
            for n in near:
                for tile in range(tiles):
                    column[j, n, tile] = jnp.broadcast_to(reach[n][tile][diag][:, off + j : off + j + 1], (8, 128))
        for n in near:
            for tile in range(tiles):
                reach[n][tile][diag] = jnp.where(inside, 0.0, reach[n][tile][diag])
        for j in range(PANEL):
            mine, at = j // 8, j % 8
            inverse = 1.0 / column[j, m, mine][at : at + 1, :]
            live = [
                (n, tile) for n in near for tile in range(tiles)
                if n > m or tile > mine or (tile == mine and at < 7)
            ]
            for k in range(j + 1, PANEL):
                factor = column[k, m, mine][at : at + 1, :] * inverse
                for n, tile in live:
                    column[k, n, tile] = column[k, n, tile] - column[j, n, tile] * factor
            for half in range(2):
                pivot_row = reach[m][mine][half][at : at + 1, :]
                if half == diag:
                    pivot_row = jnp.where(lane[0:1] == off + j, 1.0, pivot_row)
                scaled = pivot_row * inverse
                upper_ref[base + j : base + j + 1, 128 * half : 128 * half + 128] = pivot_row
                scaled_ref[base + j : base + j + 1, 128 * half : 128 * half + 128] = scaled
                for n, tile in live:
                    reach[n][tile][half] = reach[n][tile][half] - column[j, n, tile] * scaled
        del reach[m]
    row = lax.broadcasted_iota(jnp.int32, (SAMPLES, SAMPLES), 0)
    col = lax.broadcasted_iota(jnp.int32, (SAMPLES, SAMPLES), 1)
    low = col <= row
    half_solved = jnp.sum(jnp.where(low, upper_ref[...], 0.0) * target, axis=1, keepdims=True)
    return jnp.sum(jnp.where(low, scaled_ref[...], 0.0) * half_solved, axis=0, keepdims=True)


def center(joined):
    mean = jnp.sum(joined, axis=0, keepdims=True) / SAMPLES
    return ((joined - mean) * 0.0625).astype(BF16)


def kernel(
    spins_hbm, embed_hbm, position_hbm, w_hbm, bias_hbm, readout_hbm, other_hbm, energies_hbm, shift_hbm,
    coeffs_ref, update_ref, rest_ref,
    spins_ref, embed_ref, position_ref, w_ref, bias_ref, readout_ref, other_ref, energies_ref, shift_ref,
    spin_pad, table, w_pad, terms, match, spin_tile, spin_mirror, spins_all, sbuf, rbuf, cbuf, gram_part, plane_in, z_in, gram_ref, count_ref,
    upper, scaled, result, results, send_sem, recv_sem, load_sem, ready,
):
    samp, par, x, zh, y, zl, core = place()
    q = x * 4 + y
    z = zh * 4 + zl
    mine = core * 16 + q
    owner = zh == 0

    def samp_peer(step):
        dx, dz, dy = step
        nq = lax.rem(x + dx, 4) * 4 + lax.rem(y + dy, 4)
        return nq, ((nq // 4) * 8 + lax.rem(zh + dz, 2) * 4 + nq % 4, par)

    def plane_peer(step):
        dx, dy, dc = step
        nq, (to, _) = samp_peer((dx, 0, dy))
        nc = lax.rem(core + dc, 2)
        return nc * 16 + nq, (to, zl * 2 + nc)

    def z_peer(k):
        nz = lax.rem(z + k, 8)
        return (x * 8 + (nz // 4) * 4 + y, (nz % 4) * 2 + core)

    summing = (0, 1, 2, 3)
    mirror = (x * 8 + (1 - zh) * 4 + y, par)
    plane = offsets(("x", "y", "core"))
    column = (4, 3, 5, 2, 6, 1, 7)

    def summing_peer(step):
        nq, _ = samp_peer((step[0], 0, step[1]))
        return nq, ((nq // 4) * 8 + nq % 4, par)

    barrier = pltpu.get_barrier_semaphore()

    @pl.when(owner)
    def _():
        for dx, dy, _dc in [step for step in plane if step[2] == 0] + [(0, 0, 0)]:
            _, to = samp_peer((dx, 1, dy))
            pl.semaphore_signal(barrier, inc=1, device_id=to, device_id_type=MESH)
        for k in column[1:]:
            pl.semaphore_signal(barrier, inc=1, device_id=z_peer(k), device_id_type=MESH)

    for step in plane:
        pl.semaphore_signal(barrier, inc=1, device_id=plane_peer(step)[1], device_id_type=MESH)
    loads = [
        pltpu.make_async_copy(a, b, load_sem.at[n])
        for n, (a, b) in enumerate(
            (
                (spins_hbm, spins_ref), (other_hbm, other_ref), (embed_hbm, embed_ref), (position_hbm, position_ref),
                (w_hbm, w_ref), (bias_hbm, bias_ref), (readout_hbm, readout_ref),
                (energies_hbm, energies_ref), (shift_hbm, shift_ref),
            )
        )
    ]
    for load in loads:
        load.start()
    loads[0].wait()
    loads[1].wait()
    spin_pad[...] = jnp.zeros_like(spin_pad)
    spin_pad[:, 0:100] = spins_ref[...].astype(F32)
    spin_tile[...] = jnp.concatenate([spin_pad[...], jnp.zeros((8, 128), F32)], axis=0).astype(BF16)
    for n in range(16):
        sbuf[n] = jnp.concatenate(
            [other_ref[:, 128 * m : 128 * m + 128].astype(F32) for m in (2 * n, 2 * n + 1)], axis=0
        ).astype(BF16)

    @pl.when(owner)
    def _():
        pl.semaphore_wait(barrier, 34)

    @pl.when(jnp.logical_not(owner))
    def _():
        pl.semaphore_wait(barrier, 50)
        for nz in summing:
            to = (x * 8 + (nz // 4) * 4 + y, (nz % 4) * 2 + core)
            pl.semaphore_signal(ready, inc=1, device_id=to, device_id_type=MESH)

    def share(step):
        nq, to = summing_peer(step)
        pltpu.make_async_remote_copy(
            src_ref=sbuf.at[nq], dst_ref=rbuf.at[samp], send_sem=send_sem.at[0], recv_sem=recv_sem.at[0],
            device_id=to, device_id_type=MESH,
        ).start()

    @pl.when(jnp.logical_not(owner))
    def _():
        pltpu.make_async_remote_copy(
            src_ref=spin_tile, dst_ref=spin_mirror, send_sem=send_sem.at[6], recv_sem=recv_sem.at[6],
            device_id=mirror, device_id_type=MESH,
        ).start()

    for step in plane:
        if step[2] == 0:
            share(step)

    @pl.when(jnp.logical_not(owner))
    def _():
        share((0, 0))

    for load in loads[2:]:
        load.wait()

    @pl.when(owner)
    def _():
        tables(q, embed_ref, position_ref, w_ref, bias_ref, readout_ref, table, w_pad, terms, match)
        rbuf[samp] = sbuf[q]
        pltpu.make_async_copy(spin_mirror, spin_mirror, recv_sem.at[6]).wait()
        spins_all[q] = jnp.concatenate([spin_pad[...], spin_mirror[...].astype(F32)[0:8, :]], axis=0).astype(BF16)
        for step in plane:
            if step[2] == 0:
                pltpu.make_async_remote_copy(
                    src_ref=spins_all.at[q], dst_ref=spins_all.at[q], send_sem=send_sem.at[7], recv_sem=recv_sem.at[7],
                    device_id=plane_peer(step)[1], device_id_type=MESH,
                ).start()
        most = spins_all.at[pl.ds(0, 15)]
        pltpu.make_async_copy(most, most, recv_sem.at[7]).wait()
        cbuf[:, 256:384] = center(derivatives(spins_all, terms, match))
        most = rbuf.at[pl.ds(0, NSAMP - 1)]
        pltpu.make_async_copy(most, most, recv_sem.at[0]).wait()
        got = rbuf[...].astype(F32)
        for n in range(2):
            cbuf[:, 128 * n : 128 * n + 128] = center(got[:, 8 * n : 8 * n + 8, :].reshape(SAMPLES, 128))

    tiles_of = (2, 1)

    def by_core(act):
        for c in range(2):
            pl.when(core == c)(functools.partial(act, c))

    def tiles(ref, block, count):
        return ref.at[block, pl.ds(0, count)]

    @pl.when(owner)
    def _():
        product = functools.partial(
            lax.dot_general, dimension_numbers=(((1,), (1,)), ((), ())), preferred_element_type=F32
        )
        gram_part[:, 0] = product(cbuf[...], cbuf[128:256, :]).reshape(32, 8, 128)
        gram_part[0:16, 1] = product(cbuf[0:128, :], cbuf[0:128, :]).reshape(16, 8, 128)

        def reduce_plane(c):
            for step in plane:
                to, device = plane_peer(step)
                count = tiles_of[(c + step[2]) % 2]
                pltpu.make_async_remote_copy(
                    src_ref=tiles(gram_part, to, count), dst_ref=tiles(plane_in, mine, count),
                    send_sem=send_sem.at[1], recv_sem=recv_sem.at[1], device_id=device, device_id_type=MESH,
                ).start()
            count = tiles_of[c]
            plane_in[mine, 0:count] = gram_part[mine, 0:count]
            most = tiles(plane_in, pl.ds(0, 31), count)
            pltpu.make_async_copy(most, most, recv_sem.at[1]).wait()
            z_in[zl, 0:count] = jnp.sum(plane_in[:, 0:count], axis=0)

        by_core(reduce_plane)

        pl.semaphore_wait(ready, 4)

        def reduce_column(c):
            part = tiles(z_in, zl, tiles_of[c])
            for k in column:
                pltpu.make_async_remote_copy(
                    src_ref=part, dst_ref=part, send_sem=send_sem.at[2], recv_sem=recv_sem.at[2],
                    device_id=z_peer(k), device_id_type=MESH,
                ).start()
            most = tiles(z_in, pl.ds(0, 3), tiles_of[c])
            pltpu.make_async_copy(most, most, recv_sem.at[2]).wait()

        by_core(reduce_column)
        pltpu.make_async_remote_copy(
            src_ref=cbuf, dst_ref=cbuf, send_sem=send_sem.at[5], recv_sem=recv_sem.at[5],
            device_id=mirror, device_id_type=MESH,
        ).start()

    @pl.when(jnp.logical_not(owner))
    def _():
        def receive(c):
            every = tiles(z_in, pl.ds(0, 4), tiles_of[c])
            pltpu.make_async_copy(every, every, recv_sem.at[2]).wait()

        by_core(receive)

    def gather_plane(c):
        count = tiles_of[c]
        gram_ref[mine, 0:count] = jnp.sum(z_in[:, 0:count], axis=0)
        part = tiles(gram_ref, mine, count)
        for step in plane:
            pltpu.make_async_remote_copy(
                src_ref=part, dst_ref=part, send_sem=send_sem.at[3], recv_sem=recv_sem.at[3],
                device_id=plane_peer(step)[1], device_id_type=MESH,
            ).start()
        most = count_ref.at[pl.ds(0, 48 - count)]
        pltpu.make_async_copy(most, most, recv_sem.at[3]).wait()

    by_core(gather_plane)

    energies = energies_ref[...]
    target = energies - jnp.sum(energies, axis=1, keepdims=True) / SAMPLES
    x_row = solve(gram_ref, shift_ref[...], target, upper, scaled)
    coeffs_ref[...] = pltpu.roll(
        jnp.broadcast_to(x_row, (8, SAMPLES)), lax.rem(SAMPLES - OWN * samp, SAMPLES), 1
    )[0:1, 0:OWN]

    @pl.when(jnp.logical_not(owner))
    def _():
        pltpu.make_async_copy(cbuf, cbuf, recv_sem.at[5]).wait()

    first = x_row.astype(BF16).astype(F32)
    second = (x_row - first).astype(BF16).astype(F32)
    split = jnp.concatenate([first, second, x_row - first - second, jnp.zeros((13, SAMPLES), F32)], axis=0).astype(BF16)
    full = jnp.dot(split, cbuf[...], preferred_element_type=F32)
    full = full[0:1] + (full[1:2] + full[2:3])
    for n in range(3):
        result[n : n + 1, :] = full[:, 128 * n : 128 * n + 128]
    result[3:4, :] = full[:, 0:128]
    for step in plane:
        if step[2] == 0:
            pltpu.make_async_remote_copy(
                src_ref=result, dst_ref=results.at[q], send_sem=send_sem.at[4], recv_sem=recv_sem.at[4],
                device_id=plane_peer(step)[1], device_id_type=MESH,
            ).start()
    results[q] = result[...]
    most = results.at[pl.ds(0, 15)]
    pltpu.make_async_copy(most, most, recv_sem.at[4]).wait()
    rest_ref[...] = results[:, 0:2, :]
    update_ref[...] = results[:, 2, :]

    def sent(c):
        own = tiles_of[c]
        most = tiles(plane_in, pl.ds(0, 31), own)
        pltpu.make_async_copy(most, most, send_sem.at[3]).wait()

        @pl.when(owner)
        def _():
            for part, n in ((count_ref.at[pl.ds(0, 48 - own)], 1), (tiles(plane_in, pl.ds(0, 7), own), 2)):
                pltpu.make_async_copy(part, part, send_sem.at[n]).wait()

    by_core(sent)

    @pl.when(owner)
    def _():
        for part, n in ((cbuf, 5), (spins_all.at[pl.ds(0, 15)], 7)):
            pltpu.make_async_copy(part, part, send_sem.at[n]).wait()

    @pl.when(jnp.logical_not(owner))
    def _():
        for part, n in ((rbuf.at[0], 0), (spin_tile, 6)):
            pltpu.make_async_copy(part, part, send_sem.at[n]).wait()

    for part, n in ((rbuf.at[pl.ds(0, 15)], 0), (results.at[pl.ds(0, 15)], 4)):
        pltpu.make_async_copy(part, part, send_sem.at[n]).wait()


def per_device(spins, embed, position, w_first, bias_first, readout, other_grads, energies, shift):
    vmem = pl.BlockSpec(memory_space=pltpu.VMEM)
    operands = (
        spins, embed, position, w_first.T, bias_first.reshape(1, -1), readout.reshape(1, -1), other_grads,
        energies.reshape(1, -1), shift.reshape(1, 1),
    )
    operands = tuple(pltpu.with_memory_space_constraint(a, pltpu.HBM) for a in operands[:-1]) + operands[-1:]
    coeffs, update, rest = pl.pallas_call(
        kernel,
        out_shape=(
            jax.ShapeDtypeStruct((1, OWN), F32),
            jax.ShapeDtypeStruct((16, 128), F32),
            jax.ShapeDtypeStruct((16, 2, 128), F32),
        ),
        in_specs=[pl.BlockSpec(memory_space=pltpu.HBM)] * 9,
        out_specs=(vmem,) * 3,
        scratch_shapes=[pltpu.VMEM(a.shape, a.dtype) for a in operands]
        + [
            pltpu.VMEM((8, 128), F32),
            pltpu.VMEM((40, 128), F32),
            pltpu.VMEM((FOWN, 128), F32),
            pltpu.VMEM((ROWS, 384), BF16),
            pltpu.VMEM((128, ROWS), BF16),
            pltpu.VMEM((16, 128), BF16),
            pltpu.VMEM((16, 128), BF16),
            pltpu.VMEM((16, 16, 128), BF16),
            pltpu.VMEM((16, 16, 128), BF16),
            pltpu.VMEM((NSAMP, 16, 128), BF16),
            pltpu.VMEM((SAMPLES, 384), BF16),
            pltpu.VMEM((32, 2, 8, 128), F32),
            pltpu.VMEM((32, 2, 8, 128), F32),
            pltpu.VMEM((4, 2, 8, 128), F32),
            pltpu.VMEM((32, 2, 8, 128), F32),
            pltpu.VMEM((47, 8, 128), F32),
            pltpu.VMEM((SAMPLES, SAMPLES), F32),
            pltpu.VMEM((SAMPLES, SAMPLES), F32),
            pltpu.VMEM((4, 128), F32),
            pltpu.VMEM((16, 4, 128), F32),
            pltpu.SemaphoreType.DMA((8,)),
            pltpu.SemaphoreType.DMA((8,)),
            pltpu.SemaphoreType.DMA((9,)),
            pltpu.SemaphoreType.REGULAR,
        ],
        compiler_params=pltpu.CompilerParams(
            collective_id=0, has_side_effects=True, vmem_limit_bytes=32 * 2**20
        ),
        name="update",
    )(*operands)
    return (coeffs.reshape(-1), update.reshape(FOWN, D).T, rest.reshape(-1))


def solution(mesh):
    return jax.shard_map(
        per_device,
        mesh=mesh,
        in_specs=(
            P("samp", None), P(), P(), P(None, "par"), P("par"), P("par"), P("samp", "par"), P(), P(),
        ),
        out_specs=(P("samp"), P(None, "par"), P("par")),
        check_vma=False,
    )
```

```python
import itertools

import jax
import jax.numpy as jnp
from jax import lax
from jax.experimental import pallas as pl
from jax.experimental.pallas import tpu as pltpu
from jax.sharding import PartitionSpec as P

MESH = pl.DeviceIdType.MESH
HI = lax.Precision.HIGHEST
F32 = jnp.float32
BF16 = jnp.bfloat16

LSIDE = 10
PATCHES = 25
D = 64
SAMPLES = 256
OWN = 8
FOWN = 32
NSAMP = 32
NPAR = 8
NX, NZH, NY = 4, 2, 4
PANEL = 16
ROWS = 512


def place():
    samp = lax.axis_index("samp")
    par = lax.axis_index("par")
    x, zh, y = samp // 8, (samp // 4) % 2, samp % 4
    zl, core = par // 2, par % 2
    return samp, par, x, zh, y, zl, core


def site_patch(site):
    line = (site * 205) >> 11
    at = site - line * 10
    return (line >> 1) * 5 + (at >> 1), (line & 1) * 2 + (at & 1)


def patterns(shape, dim):
    pattern = lax.broadcasted_iota(jnp.int32, shape, dim) & 15
    return [jnp.where((pattern >> k) & 1 == 1, 1.0, -1.0) for k in range(4)]


def tables(q, embed_ref, position_ref, weights, table, terms, match):
    for half in (0, D):
        table[0:4, half : half + D] = embed_ref[...]
        table[8 : 8 + PATCHES, half : half + D] = position_ref[...]
    hidden = sum(sign * table[k : k + 1, :] for k, sign in enumerate(patterns((ROWS, 128), 0)))
    hidden += jnp.concatenate(
        [jnp.broadcast_to(table[8 + p : 9 + p, :], (16, 128)) for p in range(PATCHES)]
        + [jnp.zeros((ROWS - 16 * PATCHES, 128), F32)], axis=0
    )
    hidden = hidden.astype(BF16)
    lane = lax.broadcasted_iota(jnp.int32, (1, 128), 1)
    for c in range(2):
        units = jnp.concatenate(
            [jnp.broadcast_to(weights[c, pl.ds(2 * q + n, 1), :], (D, 128)) for n in range(2)], axis=0
        ).astype(BF16)

        def along(row):
            values = weights[c, row : row + 1, :]
            both = [jnp.sum(jnp.where(lane == 2 * q + n, values, 0.0), axis=1, keepdims=True) for n in range(2)]
            return jnp.where(lane < D, both[0], both[1])

        act = lax.dot_general(hidden, units, (((1,), (1,)), ((), ())), preferred_element_type=F32) + along(FOWN)
        rest = hidden.astype(F32) * (along(FOWN + 1) * jnp.tanh(act))
        for n in range(3):
            term = rest.astype(BF16)
            terms[:, 256 * n + 128 * c : 256 * n + 128 * c + 128] = term
            rest = rest - term.astype(F32)
    shape = (128, ROWS)
    patch, place_in = site_patch(lax.broadcasted_iota(jnp.int32, shape, 0))
    signs = patterns(shape, 1)
    sign = jnp.where(
        place_in == 0, signs[0], jnp.where(place_in == 1, signs[1], jnp.where(place_in == 2, signs[2], signs[3]))
    )
    match[...] = jnp.where(patch == lax.broadcasted_iota(jnp.int32, shape, 1) >> 4, sign, 0.0).astype(BF16)


def derivatives(spins_all, terms, match):
    got = spins_all[...].astype(F32)
    spins = jnp.concatenate(
        [
            got[x * 4 + y, 8 * zh : 8 * zh + 8, :]
            for x, zh, y in itertools.product(range(NX), range(NZH), range(NY))
        ], axis=0
    ).astype(BF16)
    score = jnp.dot(spins, match[...], preferred_element_type=F32)
    has = jnp.where(score > 3.5, 1.0, 0.0).astype(BF16)
    grads = jnp.dot(has, terms[...], preferred_element_type=F32)
    return grads[:, 0:256] + (grads[:, 256:512] + grads[:, 512:768])


def offsets():
    def far(step):
        return sum(min(d, 4 - d) for d in step)
    return sorted(filter(any, itertools.product(range(NX), range(NY))), key=far, reverse=True)


def solve(gram_ref, shift, target, upper_ref, scaled_ref):
    lane = lax.broadcasted_iota(jnp.int32, (8, 128), 1)
    sub = lax.broadcasted_iota(jnp.int32, (8, 128), 0)
    tiles = PANEL // 8
    panels = SAMPLES // PANEL
    reach = {}
    for m in range(panels):
        base = PANEL * m
        diag, off = base // 128, base % 128
        for n in (0, 1) if m == 0 else ((m + 1,) if m + 1 < panels else ()):
            first = PANEL * n
            owed = None
            if m:
                row = lax.broadcasted_iota(jnp.int32, (base, 128), 0)
                col = lax.broadcasted_iota(jnp.int32, (base, 128), 1)
                right = []
                for half in range(2):
                    part = scaled_ref[0:base, 128 * half : 128 * half + 128]
                    if half < diag:
                        part = jnp.where(col + 128 * half <= row, part, 0.0)
                    elif half == diag:
                        part = jnp.where((col >= off) | (col + 128 * half <= row), part, 0.0)
                    right.append(part)
                owed = lax.dot_general(
                    upper_ref[0:base, first : first + PANEL], jnp.concatenate(right, axis=1),
                    (((0,), (0,)), ((), ())), preferred_element_type=F32, precision=HI,
                )
            rows = []
            for tile in range(tiles):
                pair = []
                for half in range(2):
                    part = gram_ref[first // PANEL, tile, :, 128 * half : 128 * half + 128]
                    at = first + 8 * tile - 128 * half
                    if 0 <= at < 128:
                        part = jnp.where(lane == sub + at, part + shift, part)
                    if half < diag:
                        part = jnp.zeros_like(part)
                    elif half == diag and off:
                        part = jnp.where(lane >= off, part, 0.0)
                    if owed is not None:
                        part = part - owed[8 * tile : 8 * tile + 8, 128 * half : 128 * half + 128]
                    pair.append(part)
                rows.append(pair)
            reach[n] = rows
        near = [n for n in (m, m + 1) if n < panels]
        inside = (lane >= off) & (lane < off + PANEL)
        column = {}
        for j in range(PANEL):
            for n in near:
                for tile in range(tiles):
                    column[j, n, tile] = jnp.broadcast_to(reach[n][tile][diag][:, off + j : off + j + 1], (8, 128))
        for n in near:
            for tile in range(tiles):
                reach[n][tile][diag] = jnp.where(inside, 0.0, reach[n][tile][diag])
        for j in range(PANEL):
            mine, at = j // 8, j % 8
            inverse = 1.0 / column[j, m, mine][at : at + 1, :]
            live = [
                (n, tile) for n in near for tile in range(tiles)
                if n > m or tile > mine or (tile == mine and at < 7)
            ]
            for k in range(j + 1, PANEL):
                factor = column[k, m, mine][at : at + 1, :] * inverse
                for n, tile in live:
                    column[k, n, tile] = column[k, n, tile] - column[j, n, tile] * factor
            for half in range(2):
                pivot_row = reach[m][mine][half][at : at + 1, :]
                if half == diag:
                    pivot_row = jnp.where(lane[0:1] == off + j, 1.0, pivot_row)
                scaled = pivot_row * inverse
                upper_ref[base + j : base + j + 1, 128 * half : 128 * half + 128] = pivot_row
                scaled_ref[base + j : base + j + 1, 128 * half : 128 * half + 128] = scaled
                for n, tile in live:
                    reach[n][tile][half] = reach[n][tile][half] - column[j, n, tile] * scaled
        del reach[m]
    row = lax.broadcasted_iota(jnp.int32, (SAMPLES, SAMPLES), 0)
    col = lax.broadcasted_iota(jnp.int32, (SAMPLES, SAMPLES), 1)
    low = col <= row
    half_solved = jnp.sum(jnp.where(low, upper_ref[...], 0.0) * target, axis=1, keepdims=True)
    return jnp.sum(jnp.where(low, scaled_ref[...], 0.0) * half_solved, axis=0, keepdims=True)


def center(joined):
    mean = jnp.sum(joined, axis=0, keepdims=True) / SAMPLES
    return ((joined - mean) * 0.0625).astype(BF16)


def kernel(
    spins_hbm, other_hbm, embed_hbm, position_hbm, w_hbm, bias_hbm, readout_hbm, energies_hbm, shift_hbm,
    coeffs_ref, update_ref, rest_ref,
    spins_ref, other_ref, embed_ref, position_ref, w_ref, bias_ref, readout_ref, energies_ref, shift_ref,
    spin_pad, table, weights, terms, match, spin_tile, spin_mirror, spins_all, sbuf, rbuf, cbuf,
    gram_part, plane_in, z_in, gram_ref, upper, scaled, x_buf, result, results, send_sem, recv_sem, load_sem, ready,
):
    samp, par, x, zh, y, zl, core = place()
    q = x * 4 + y
    z = zh * 4 + zl
    lead = core == 1
    follow = jnp.logical_not(lead)
    summing = jnp.logical_and(lead, zh == 0)
    idle = jnp.logical_and(lead, zh == 1)

    def device(nq, nzh, nzl, ncore):
        return ((nq // 4) * 8 + nzh * 4 + nq % 4, nzl * 2 + ncore)

    def beside(step):
        return lax.rem(x + step[0], 4) * 4 + lax.rem(y + step[1], 4)

    def along_z(nz):
        return device(q, nz // 4, nz % 4, 1)

    def send(src, dst, n, to):
        pltpu.make_async_remote_copy(
            src_ref=src, dst_ref=dst, send_sem=send_sem.at[n], recv_sem=recv_sem.at[n], device_id=to, device_id_type=MESH
        ).start()

    def came(part, n):
        pltpu.make_async_copy(part, part, recv_sem.at[n]).wait()

    def left(part, n):
        pltpu.make_async_copy(part, part, send_sem.at[n]).wait()

    plane = offsets()
    mate = device(q, zh, zl, 1 - core)
    mirror = device(q, 1 - zh, zl, 1)

    barrier = pltpu.get_barrier_semaphore()

    def greet(to):
        pl.semaphore_signal(barrier, inc=1, device_id=to, device_id_type=MESH)

    @pl.when(summing)
    def _():
        for step in plane + [(0, 0)]:
            for c in (0, 1):
                greet(device(beside(step), 1, zl, c))
        for k in (3, 5, 2, 6, 1, 7):
            greet(along_z(lax.rem(z + k, 8)))
        for step in plane:
            for c in (0, 1):
                greet(device(beside(step), 0, zl, c))

    @pl.when(idle)
    def _():
        for step in plane:
            greet(device(beside(step), 1, zl, 1))

    greet(mate)

    loads = [
        pltpu.make_async_copy(a, b, load_sem.at[n])
        for n, (a, b) in enumerate(
            (
                (spins_hbm, spins_ref), (other_hbm, other_ref), (embed_hbm, embed_ref), (position_hbm, position_ref),
                (w_hbm, w_ref), (bias_hbm, bias_ref), (readout_hbm, readout_ref),
                (energies_hbm, energies_ref), (shift_hbm, shift_ref),
            )
        )
    ]
    for load in loads:
        load.start()
    for load in loads:
        load.wait()
    spin_pad[...] = jnp.zeros_like(spin_pad)
    spin_pad[:, 0:100] = spins_ref[...].astype(F32)
    spin_tile[...] = jnp.concatenate([spin_pad[...], jnp.zeros((8, 128), F32)], axis=0).astype(BF16)
    for n in range(16):
        sbuf[n] = jnp.concatenate(
            [other_ref[:, 128 * m : 128 * m + 128].astype(F32) for m in (2 * n, 2 * n + 1)], axis=0
        ).astype(BF16)
    weights[core] = jnp.zeros((40, 128), F32)
    weights[core, 0:FOWN, 0:D] = w_ref[...].astype(F32)
    weights[core, FOWN : FOWN + 1, 0:FOWN] = bias_ref[...]
    weights[core, FOWN + 1 : FOWN + 2, 0:FOWN] = readout_ref[...]

    def share(step):
        nq = beside(step)
        send(sbuf.at[nq], rbuf.at[core * NSAMP + samp], 0, device(nq, 0, zl, 1))

    @pl.when(summing)
    def _():
        pl.semaphore_wait(barrier, 19)
        for step in plane:
            share(step)

    @pl.when(idle)
    def _():
        pl.semaphore_wait(barrier, 35)
        send(spin_tile, spin_mirror, 6, mirror)
        for step in plane + [(0, 0)]:
            share(step)
        for nz in range(4):
            pl.semaphore_signal(ready, inc=1, device_id=along_z(nz), device_id_type=MESH)

    @pl.when(jnp.logical_and(follow, zh == 0))
    def _():
        pl.semaphore_wait(barrier, 16)
        for step in plane + [(0, 0)]:
            share(step)
        send(weights.at[0], weights.at[0], 8, mate)

    @pl.when(jnp.logical_and(follow, zh == 1))
    def _():
        pl.semaphore_wait(barrier, 17)
        for step in plane + [(0, 0)]:
            share(step)

    @pl.when(summing)
    def _():
        came(weights.at[0], 8)
        tables(q, embed_ref, position_ref, weights, table, terms, match)
        rbuf[NSAMP + samp] = sbuf[q]
        came(spin_mirror, 6)
        spins_all[q] = jnp.concatenate([spin_pad[...], spin_mirror[...].astype(F32)[0:8, :]], axis=0).astype(BF16)
        for step in plane:
            send(spins_all.at[q], spins_all.at[q], 7, device(beside(step), 0, zl, 1))
        came(spins_all.at[pl.ds(0, 15)], 7)
        cbuf[:, 512:768] = center(derivatives(spins_all, terms, match))
        came(rbuf.at[pl.ds(0, 2 * NSAMP - 1)], 0)
        for c in range(2):
            got = rbuf[NSAMP * c : NSAMP * (c + 1)].astype(F32)
            for n in range(2):
                at = 256 * c + 128 * n
                cbuf[:, at : at + 128] = center(got[:, 8 * n : 8 * n + 8, :].reshape(SAMPLES, 128))

        gram_part[...] = lax.dot_general(
            cbuf[...], cbuf[...], (((1,), (1,)), ((), ())), preferred_element_type=F32
        ).reshape(16, 2, 8, SAMPLES)
        for step in plane:
            nq = beside(step)
            send(gram_part.at[nq], plane_in.at[q], 1, device(nq, 0, zl, 1))
        plane_in[q] = gram_part[q]
        came(plane_in.at[pl.ds(0, 15)], 1)
        z_in[zl] = jnp.sum(plane_in[...], axis=0)

        pl.semaphore_wait(ready, 4)
        for k in (4, 3, 5, 2, 6, 1, 7):
            send(z_in.at[zl], z_in.at[zl], 2, along_z(lax.rem(z + k, 8)))
        came(z_in.at[pl.ds(0, 3)], 2)
        send(cbuf, cbuf, 5, mirror)

    @pl.when(idle)
    def _():
        came(z_in, 2)

    @pl.when(lead)
    def _():
        gram_ref[q] = jnp.sum(z_in[...], axis=0)
        for step in plane:
            send(gram_ref.at[q], gram_ref.at[q], 3, device(beside(step), zh, zl, 1))
        came(gram_ref.at[pl.ds(0, 15)], 3)

        energies = energies_ref[...]
        target = energies - jnp.sum(energies, axis=1, keepdims=True) / SAMPLES
        x_row = solve(gram_ref, shift_ref[...], target, upper, scaled)
        x_buf[...] = jnp.broadcast_to(x_row, (8, SAMPLES))
        send(x_buf, x_buf, 9, mate)

        @pl.when(zh == 1)
        def _():
            came(cbuf, 5)

        first = x_row.astype(BF16).astype(F32)
        second = (x_row - first).astype(BF16).astype(F32)
        split = jnp.concatenate(
            [first, second, x_row - first - second, jnp.zeros((13, SAMPLES), F32)], axis=0
        ).astype(BF16)
        full = jnp.dot(split, cbuf[...], preferred_element_type=F32)
        full = full[0:1] + (full[1:2] + full[2:3])
        result[...] = jnp.zeros_like(result)
        for n, row in enumerate((0, 1, 3, 4, 2, 5)):
            result[row : row + 1, :] = full[:, 128 * n : 128 * n + 128]
        for step in plane:
            send(result, results.at[q], 4, device(beside(step), zh, zl, 1))
        results[q] = result[...]
        came(results.at[pl.ds(0, 15)], 4)
        send(results, results, 10, mate)

    @pl.when(follow)
    def _():
        came(x_buf, 9)
        came(results, 10)

    coeffs_ref[...] = pltpu.roll(x_buf[...], lax.rem(SAMPLES - OWN * samp, SAMPLES), 1)[0:1, 0:OWN]
    for c in range(2):
        @pl.when(core == c)
        def _():
            rest_ref[...] = results[:, 3 * c : 3 * c + 2, :]
            update_ref[...] = results[:, 3 * c + 2, :]

    @pl.when(lead)
    def _():
        for part, n in ((gram_ref.at[pl.ds(0, 15)], 3), (results.at[pl.ds(0, 15)], 4), (x_buf, 9), (results, 10)):
            left(part, n)

    @pl.when(summing)
    def _():
        for part, n in (
            (rbuf.at[pl.ds(0, 15)], 0), (plane_in.at[pl.ds(0, 15)], 1), (plane_in.at[pl.ds(0, 7)], 2), (cbuf, 5),
            (spins_all.at[pl.ds(0, 15)], 7),
        ):
            left(part, n)

    @pl.when(jnp.logical_not(summing))
    def _():
        left(rbuf.at[pl.ds(0, 16)], 0)

    @pl.when(idle)
    def _():
        left(spin_tile, 6)

    @pl.when(jnp.logical_and(follow, zh == 0))
    def _():
        left(weights.at[0], 8)


def per_device(spins, embed, position, w_first, bias_first, readout, other_grads, energies, shift):
    vmem = pl.BlockSpec(memory_space=pltpu.VMEM)
    operands = (
        spins, other_grads, embed, position, w_first.T, bias_first.reshape(1, -1), readout.reshape(1, -1),
        energies.reshape(1, -1), shift.reshape(1, 1),
    )
    operands = tuple(pltpu.with_memory_space_constraint(a, pltpu.HBM) for a in operands[:-1]) + operands[-1:]
    coeffs, update, rest = pl.pallas_call(
        kernel,
        out_shape=(
            jax.ShapeDtypeStruct((1, OWN), F32),
            jax.ShapeDtypeStruct((16, 128), F32),
            jax.ShapeDtypeStruct((16, 2, 128), F32),
        ),
        in_specs=[pl.BlockSpec(memory_space=pltpu.HBM)] * 9,
        out_specs=(vmem,) * 3,
        scratch_shapes=[pltpu.VMEM(a.shape, a.dtype) for a in operands]
        + [
            pltpu.VMEM((8, 128), F32),
            pltpu.VMEM((40, 128), F32),
            pltpu.VMEM((2, 40, 128), F32),
            pltpu.VMEM((ROWS, 768), BF16),
            pltpu.VMEM((128, ROWS), BF16),
            pltpu.VMEM((16, 128), BF16),
            pltpu.VMEM((16, 128), BF16),
            pltpu.VMEM((16, 16, 128), BF16),
            pltpu.VMEM((16, 16, 128), BF16),
            pltpu.VMEM((2 * NSAMP, 16, 128), BF16),
            pltpu.VMEM((SAMPLES, 768), BF16),
            pltpu.VMEM((16, 2, 8, SAMPLES), F32),
            pltpu.VMEM((16, 2, 8, SAMPLES), F32),
            pltpu.VMEM((4, 2, 8, SAMPLES), F32),
            pltpu.VMEM((16, 2, 8, SAMPLES), F32),
            pltpu.VMEM((SAMPLES, SAMPLES), F32),
            pltpu.VMEM((SAMPLES, SAMPLES), F32),
            pltpu.VMEM((8, SAMPLES), F32),
            pltpu.VMEM((8, 128), F32),
            pltpu.VMEM((16, 8, 128), F32),
            pltpu.SemaphoreType.DMA((11,)),
            pltpu.SemaphoreType.DMA((11,)),
            pltpu.SemaphoreType.DMA((9,)),
            pltpu.SemaphoreType.REGULAR,
        ],
        compiler_params=pltpu.CompilerParams(
            collective_id=0, has_side_effects=True, vmem_limit_bytes=32 * 2**20
        ),
        name="update",
    )(*operands)
    return (coeffs.reshape(-1), update.reshape(FOWN, D).T, rest.reshape(-1))


def solution(mesh):
    return jax.shard_map(
        per_device,
        mesh=mesh,
        in_specs=(
            P("samp", None), P(), P(), P(None, "par"), P("par"), P("par"), P("samp", "par"), P(), P(),
        ),
        out_specs=(P("samp"), P(None, "par"), P("par")),
        check_vma=False,
    )
```

```python
import itertools

import jax
import jax.numpy as jnp
from jax import lax
from jax.experimental import pallas as pl
from jax.experimental.pallas import tpu as pltpu
from jax.sharding import PartitionSpec as P

MESH = pl.DeviceIdType.MESH
HI = lax.Precision.HIGHEST
F32 = jnp.float32
BF16 = jnp.bfloat16

LSIDE = 10
PATCHES = 25
D = 64
SAMPLES = 256
OWN = 8
FOWN = 32
NSAMP = 32
NPAR = 8
NX, NZH, NY = 4, 2, 4
PANEL = 16
ROWS = 512


def place():
    samp = lax.axis_index("samp")
    par = lax.axis_index("par")
    x, zh, y = samp // 8, (samp // 4) % 2, samp % 4
    zl, core = par // 2, par % 2
    return samp, par, x, zh, y, zl, core


def site_patch(site):
    line = (site * 205) >> 11
    at = site - line * 10
    return (line >> 1) * 5 + (at >> 1), (line & 1) * 2 + (at & 1)


def patterns(shape, dim):
    pattern = lax.broadcasted_iota(jnp.int32, shape, dim) & 15
    return [jnp.where((pattern >> k) & 1 == 1, 1.0, -1.0) for k in range(4)]


def tables(q, embed_ref, position_ref, weights, table, terms, match):
    for half in (0, D):
        table[0:4, half : half + D] = embed_ref[...]
        table[8 : 8 + PATCHES, half : half + D] = position_ref[...]
    hidden = sum(sign * table[k : k + 1, :] for k, sign in enumerate(patterns((ROWS, 128), 0)))
    hidden += jnp.concatenate(
        [jnp.broadcast_to(table[8 + p : 9 + p, :], (16, 128)) for p in range(PATCHES)]
        + [jnp.zeros((ROWS - 16 * PATCHES, 128), F32)], axis=0
    )
    hidden = hidden.astype(BF16)
    lane = lax.broadcasted_iota(jnp.int32, (1, 128), 1)
    for c in range(2):
        units = jnp.concatenate(
            [jnp.broadcast_to(weights[c, pl.ds(2 * q + n, 1), :], (D, 128)) for n in range(2)], axis=0
        ).astype(BF16)

        def along(row):
            values = weights[c, row : row + 1, :]
            both = [jnp.sum(jnp.where(lane == 2 * q + n, values, 0.0), axis=1, keepdims=True) for n in range(2)]
            return jnp.where(lane < D, both[0], both[1])

        act = lax.dot_general(hidden, units, (((1,), (1,)), ((), ())), preferred_element_type=F32) + along(FOWN)
        rest = hidden.astype(F32) * (along(FOWN + 1) * jnp.tanh(act))
        for n in range(3):
            term = rest.astype(BF16)
            terms[:, 256 * n + 128 * c : 256 * n + 128 * c + 128] = term
            rest = rest - term.astype(F32)
    shape = (128, ROWS)
    patch, place_in = site_patch(lax.broadcasted_iota(jnp.int32, shape, 0))
    signs = patterns(shape, 1)
    sign = jnp.where(
        place_in == 0, signs[0], jnp.where(place_in == 1, signs[1], jnp.where(place_in == 2, signs[2], signs[3]))
    )
    match[...] = jnp.where(patch == lax.broadcasted_iota(jnp.int32, shape, 1) >> 4, sign, 0.0).astype(BF16)


def derivatives(spins_all, terms, match):
    got = spins_all[...].astype(F32)
    spins = jnp.concatenate(
        [
            got[x * 4 + y, 8 * zh : 8 * zh + 8, :]
            for x, zh, y in itertools.product(range(NX), range(NZH), range(NY))
        ], axis=0
    ).astype(BF16)
    score = jnp.dot(spins, match[...], preferred_element_type=F32)
    has = jnp.where(score > 3.5, 1.0, 0.0).astype(BF16)
    grads = jnp.dot(has, terms[...], preferred_element_type=F32)
    return grads[:, 0:256] + (grads[:, 256:512] + grads[:, 512:768])


def offsets():
    def far(step):
        return sum(min(d, 4 - d) for d in step)
    return sorted(filter(any, itertools.product(range(NX), range(NY))), key=far, reverse=True)


def solve(gram_ref, shift, target, upper_ref, scaled_ref):
    lane = lax.broadcasted_iota(jnp.int32, (8, 128), 1)
    sub = lax.broadcasted_iota(jnp.int32, (8, 128), 0)
    tiles = PANEL // 8
    panels = SAMPLES // PANEL
    reach = {}
    for m in range(panels):
        base = PANEL * m
        diag, off = base // 128, base % 128
        for n in (0, 1) if m == 0 else ((m + 1,) if m + 1 < panels else ()):
            first = PANEL * n
            owed = None
            if m:
                row = lax.broadcasted_iota(jnp.int32, (base, 128), 0)
                col = lax.broadcasted_iota(jnp.int32, (base, 128), 1)
                right = []
                for half in range(2):
                    part = scaled_ref[0:base, 128 * half : 128 * half + 128]
                    if half < diag:
                        part = jnp.where(col + 128 * half <= row, part, 0.0)
                    elif half == diag:
                        part = jnp.where((col >= off) | (col + 128 * half <= row), part, 0.0)
                    right.append(part)
                owed = lax.dot_general(
                    upper_ref[0:base, first : first + PANEL], jnp.concatenate(right, axis=1),
                    (((0,), (0,)), ((), ())), preferred_element_type=F32, precision=HI,
                )
            rows = []
            for tile in range(tiles):
                pair = []
                for half in range(2):
                    part = gram_ref[first // PANEL, tile, :, 128 * half : 128 * half + 128]
                    at = first + 8 * tile - 128 * half
                    if 0 <= at < 128:
                        part = jnp.where(lane == sub + at, part + shift, part)
                    if half < diag:
                        part = jnp.zeros_like(part)
                    elif half == diag and off:
                        part = jnp.where(lane >= off, part, 0.0)
                    if owed is not None:
                        part = part - owed[8 * tile : 8 * tile + 8, 128 * half : 128 * half + 128]
                    pair.append(part)
                rows.append(pair)
            reach[n] = rows
        near = [n for n in (m, m + 1) if n < panels]
        inside = (lane >= off) & (lane < off + PANEL)
        column = {}
        for j in range(PANEL):
            for n in near:
                for tile in range(tiles):
                    column[j, n, tile] = jnp.broadcast_to(reach[n][tile][diag][:, off + j : off + j + 1], (8, 128))
        for n in near:
            for tile in range(tiles):
                reach[n][tile][diag] = jnp.where(inside, 0.0, reach[n][tile][diag])
        for j in range(PANEL):
            mine, at = j // 8, j % 8
            inverse = 1.0 / column[j, m, mine][at : at + 1, :]
            live = [
                (n, tile) for n in near for tile in range(tiles)
                if n > m or tile > mine or (tile == mine and at < 7)
            ]
            for k in range(j + 1, PANEL):
                factor = column[k, m, mine][at : at + 1, :] * inverse
                for n, tile in live:
                    column[k, n, tile] = column[k, n, tile] - column[j, n, tile] * factor
            for half in range(2):
                pivot_row = reach[m][mine][half][at : at + 1, :]
                if half == diag:
                    pivot_row = jnp.where(lane[0:1] == off + j, 1.0, pivot_row)
                scaled = pivot_row * inverse
                upper_ref[base + j : base + j + 1, 128 * half : 128 * half + 128] = pivot_row
                scaled_ref[base + j : base + j + 1, 128 * half : 128 * half + 128] = scaled
                for n, tile in live:
                    reach[n][tile][half] = reach[n][tile][half] - column[j, n, tile] * scaled
        del reach[m]
    row = lax.broadcasted_iota(jnp.int32, (SAMPLES, SAMPLES), 0)
    col = lax.broadcasted_iota(jnp.int32, (SAMPLES, SAMPLES), 1)
    low = col <= row
    half_solved = jnp.sum(jnp.where(low, upper_ref[...], 0.0) * target, axis=1, keepdims=True)
    return jnp.sum(jnp.where(low, scaled_ref[...], 0.0) * half_solved, axis=0, keepdims=True)


def center(joined):
    mean = jnp.sum(joined, axis=0, keepdims=True) / SAMPLES
    return ((joined - mean) * 0.0625).astype(BF16)


def kernel(
    spins_hbm, other_hbm, embed_hbm, position_hbm, w_hbm, bias_hbm, readout_hbm, energies_hbm, shift_hbm,
    coeffs_ref, update_ref, rest_ref,
    spins_ref, other_ref, embed_ref, position_ref, w_ref, bias_ref, readout_ref, energies_ref, shift_ref,
    spin_pad, table, weights, terms, match, spin_tile, spin_mirror, spins_all, sbuf, rbuf, cbuf,
    gram_part, plane_in, z_in, gram_ref, upper, scaled, x_buf, result, results, send_sem, recv_sem, load_sem, ready,
):
    samp, par, x, zh, y, zl, core = place()
    q = x * 4 + y
    z = zh * 4 + zl
    lead = core == 1
    follow = jnp.logical_not(lead)
    summing = jnp.logical_and(lead, zh == 0)
    idle = jnp.logical_and(lead, zh == 1)

    def device(nq, nzh, nzl, ncore):
        return ((nq // 4) * 8 + nzh * 4 + nq % 4, nzl * 2 + ncore)

    def beside(step):
        return lax.rem(x + step[0], 4) * 4 + lax.rem(y + step[1], 4)

    def along_z(nz):
        return device(q, nz // 4, nz % 4, 1)

    def send(src, dst, n, to):
        pltpu.make_async_remote_copy(
            src_ref=src, dst_ref=dst, send_sem=send_sem.at[n], recv_sem=recv_sem.at[n], device_id=to, device_id_type=MESH
        ).start()

    def came(part, n):
        pltpu.make_async_copy(part, part, recv_sem.at[n]).wait()

    def left(part, n):
        pltpu.make_async_copy(part, part, send_sem.at[n]).wait()

    plane = offsets()
    mate = device(q, zh, zl, 1 - core)
    mirror = device(q, 1 - zh, zl, 1)

    barrier = pltpu.get_barrier_semaphore()

    def greet(to):
        pl.semaphore_signal(barrier, inc=1, device_id=to, device_id_type=MESH)

    @pl.when(summing)
    def _():
        for step in plane + [(0, 0)]:
            for c in (0, 1):
                greet(device(beside(step), 1, zl, c))
        for k in (3, 5, 2, 6, 1, 7):
            greet(along_z(lax.rem(z + k, 8)))
        for step in plane:
            for c in (0, 1):
                greet(device(beside(step), 0, zl, c))

    @pl.when(idle)
    def _():
        for step in plane:
            greet(device(beside(step), 1, zl, 1))

    @pl.when(follow)
    def _():
        for step in plane:
            greet(device(beside(step), zh, zl, 1))

    greet(mate)

    loads = [
        pltpu.make_async_copy(a, b, load_sem.at[n])
        for n, (a, b) in enumerate(
            (
                (spins_hbm, spins_ref), (other_hbm, other_ref), (embed_hbm, embed_ref), (position_hbm, position_ref),
                (w_hbm, w_ref), (bias_hbm, bias_ref), (readout_hbm, readout_ref),
                (energies_hbm, energies_ref), (shift_hbm, shift_ref),
            )
        )
    ]
    for load in loads:
        load.start()
    for load in loads:
        load.wait()
    spin_pad[...] = jnp.zeros_like(spin_pad)
    spin_pad[:, 0:100] = spins_ref[...].astype(F32)
    spin_tile[...] = jnp.concatenate([spin_pad[...], jnp.zeros((8, 128), F32)], axis=0).astype(BF16)
    for n in range(16):
        sbuf[n] = jnp.concatenate(
            [other_ref[:, 128 * m : 128 * m + 128].astype(F32) for m in (2 * n, 2 * n + 1)], axis=0
        ).astype(BF16)
    weights[core] = jnp.zeros((40, 128), F32)
    weights[core, 0:FOWN, 0:D] = w_ref[...].astype(F32)
    weights[core, FOWN : FOWN + 1, 0:FOWN] = bias_ref[...]
    weights[core, FOWN + 1 : FOWN + 2, 0:FOWN] = readout_ref[...]

    def share(step):
        nq = beside(step)
        send(sbuf.at[nq], rbuf.at[core * NSAMP + samp], 0, device(nq, 0, zl, 1))

    @pl.when(summing)
    def _():
        pl.semaphore_wait(barrier, 34)
        for step in plane:
            share(step)

    @pl.when(idle)
    def _():
        pl.semaphore_wait(barrier, 50)
        send(spin_tile, spin_mirror, 6, mirror)
        for step in plane + [(0, 0)]:
            share(step)
        for nz in range(4):
            pl.semaphore_signal(ready, inc=1, device_id=along_z(nz), device_id_type=MESH)

    @pl.when(jnp.logical_and(follow, zh == 0))
    def _():
        pl.semaphore_wait(barrier, 16)
        for step in plane + [(0, 0)]:
            share(step)
        send(weights.at[0], weights.at[0], 8, mate)

    @pl.when(jnp.logical_and(follow, zh == 1))
    def _():
        pl.semaphore_wait(barrier, 17)
        for step in plane + [(0, 0)]:
            share(step)

    @pl.when(summing)
    def _():
        came(weights.at[0], 8)
        tables(q, embed_ref, position_ref, weights, table, terms, match)
        rbuf[NSAMP + samp] = sbuf[q]
        came(spin_mirror, 6)
        spins_all[q] = jnp.concatenate([spin_pad[...], spin_mirror[...].astype(F32)[0:8, :]], axis=0).astype(BF16)
        for step in plane:
            send(spins_all.at[q], spins_all.at[q], 7, device(beside(step), 0, zl, 1))
        came(spins_all.at[pl.ds(0, 15)], 7)
        cbuf[:, 512:768] = center(derivatives(spins_all, terms, match))

        def products(columns):
            return lax.dot_general(columns, columns, (((1,), (1,)), ((), ())), preferred_element_type=F32)

        gram_part[...] = products(cbuf[:, 512:768]).reshape(16, 2, 8, SAMPLES)
        came(rbuf.at[pl.ds(0, 2 * NSAMP - 1)], 0)
        for c in range(2):
            got = rbuf[NSAMP * c : NSAMP * (c + 1)].astype(F32)
            for n in range(2):
                at = 256 * c + 128 * n
                cbuf[:, at : at + 128] = center(got[:, 8 * n : 8 * n + 8, :].reshape(SAMPLES, 128))

        gram_part[...] += products(cbuf[:, 0:512]).reshape(16, 2, 8, SAMPLES)
        for step in plane:
            nq = beside(step)
            send(gram_part.at[nq], plane_in.at[q], 1, device(nq, 0, zl, 1))
        plane_in[q] = gram_part[q]
        came(plane_in.at[pl.ds(0, 15)], 1)
        z_in[zl] = jnp.sum(plane_in[...], axis=0)

        pl.semaphore_wait(ready, 4)
        for k in (4, 3, 5, 2, 6, 1, 7):
            send(z_in.at[zl], z_in.at[zl], 2, along_z(lax.rem(z + k, 8)))
        came(z_in.at[pl.ds(0, 3)], 2)
        send(cbuf, cbuf, 5, mirror)

    @pl.when(idle)
    def _():
        came(z_in, 2)

    @pl.when(lead)
    def _():
        gram_ref[q] = jnp.sum(z_in[...], axis=0)
        for step in plane:
            send(gram_ref.at[q], gram_ref.at[q], 3, device(beside(step), zh, zl, 1))
        energies = energies_ref[...]
        target = energies - jnp.sum(energies, axis=1, keepdims=True) / SAMPLES
        came(gram_ref.at[pl.ds(0, 15)], 3)

        x_row = solve(gram_ref, shift_ref[...], target, upper, scaled)
        x_buf[...] = jnp.broadcast_to(x_row, (8, SAMPLES))
        send(x_buf, x_buf, 9, mate)

        @pl.when(zh == 1)
        def _():
            came(cbuf, 5)

        first = x_row.astype(BF16).astype(F32)
        second = (x_row - first).astype(BF16).astype(F32)
        split = jnp.concatenate(
            [first, second, x_row - first - second, jnp.zeros((13, SAMPLES), F32)], axis=0
        ).astype(BF16)
        full = jnp.dot(split, cbuf[...], preferred_element_type=F32)
        full = full[0:1] + (full[1:2] + full[2:3])
        result[...] = jnp.zeros_like(result)
        for n, (c, row) in enumerate(((0, 0), (0, 1), (1, 0), (1, 1), (0, 2), (1, 2))):
            result[c, row : row + 1, :] = full[:, 128 * n : 128 * n + 128]
        for step in plane:
            send(result.at[1], results.at[q], 4, device(beside(step), zh, zl, 1))
        for step in plane + [(0, 0)]:
            send(result.at[0], results.at[q], 4, device(beside(step), zh, zl, 0))
        results[q] = result[1]
        came(results.at[pl.ds(0, 15)], 4)

    @pl.when(follow)
    def _():
        came(x_buf, 9)
        came(results, 4)

    coeffs_ref[...] = pltpu.roll(x_buf[...], lax.rem(SAMPLES - OWN * samp, SAMPLES), 1)[0:1, 0:OWN]
    rest_ref[...] = results[:, 0:2, :]
    layer = results[:, 2, :]
    update_ref[:, 0, :] = layer[:, 0:D]
    update_ref[:, 1, :] = pltpu.roll(layer, D, 1)[:, 0:D]

    @pl.when(lead)
    def _():
        for part, n in ((gram_ref.at[pl.ds(0, 15)], 3), (results, 4), (results.at[pl.ds(0, 15)], 4), (x_buf, 9)):
            left(part, n)

    @pl.when(summing)
    def _():
        for part, n in (
            (rbuf.at[pl.ds(0, 15)], 0), (plane_in.at[pl.ds(0, 15)], 1), (plane_in.at[pl.ds(0, 7)], 2), (cbuf, 5),
            (spins_all.at[pl.ds(0, 15)], 7),
        ):
            left(part, n)

    @pl.when(jnp.logical_not(summing))
    def _():
        left(rbuf.at[pl.ds(0, 16)], 0)

    @pl.when(idle)
    def _():
        left(spin_tile, 6)

    @pl.when(jnp.logical_and(follow, zh == 0))
    def _():
        left(weights.at[0], 8)


def write_out(coeffs, update, rest, coeffs_out, update_out, rest_out, sem):
    copies = [
        pltpu.make_async_copy(a, b, sem.at[n])
        for n, (a, b) in enumerate(((rest, rest_out), (update, update_out), (coeffs, coeffs_out)))
    ]
    for copy in copies:
        copy.start()
    for copy in copies:
        copy.wait()


def per_device(spins, embed, position, w_first, bias_first, readout, other_grads, energies, shift):
    vmem = pl.BlockSpec(memory_space=pltpu.VMEM)
    operands = (
        spins, other_grads, embed, position, w_first.T, bias_first.reshape(1, -1), readout.reshape(1, -1),
        energies.reshape(1, -1), shift.reshape(1, 1),
    )
    operands = tuple(pltpu.with_memory_space_constraint(a, pltpu.HBM) for a in operands[:-1]) + operands[-1:]
    coeffs, update, rest = pl.pallas_call(
        kernel,
        out_shape=(
            jax.ShapeDtypeStruct((1, OWN), F32),
            jax.ShapeDtypeStruct((16, 2, D), F32),
            jax.ShapeDtypeStruct((16, 2, 128), F32),
        ),
        in_specs=[pl.BlockSpec(memory_space=pltpu.HBM)] * 9,
        out_specs=(vmem,) * 3,
        scratch_shapes=[pltpu.VMEM(a.shape, a.dtype) for a in operands]
        + [
            pltpu.VMEM((8, 128), F32),
            pltpu.VMEM((40, 128), F32),
            pltpu.VMEM((2, 40, 128), F32),
            pltpu.VMEM((ROWS, 768), BF16),
            pltpu.VMEM((128, ROWS), BF16),
            pltpu.VMEM((16, 128), BF16),
            pltpu.VMEM((16, 128), BF16),
            pltpu.VMEM((16, 16, 128), BF16),
            pltpu.VMEM((16, 16, 128), BF16),
            pltpu.VMEM((2 * NSAMP, 16, 128), BF16),
            pltpu.VMEM((SAMPLES, 768), BF16),
            pltpu.VMEM((16, 2, 8, SAMPLES), F32),
            pltpu.VMEM((16, 2, 8, SAMPLES), F32),
            pltpu.VMEM((4, 2, 8, SAMPLES), F32),
            pltpu.VMEM((16, 2, 8, SAMPLES), F32),
            pltpu.VMEM((SAMPLES, SAMPLES), F32),
            pltpu.VMEM((SAMPLES, SAMPLES), F32),
            pltpu.VMEM((8, SAMPLES), F32),
            pltpu.VMEM((2, 4, 128), F32),
            pltpu.VMEM((16, 4, 128), F32),
            pltpu.SemaphoreType.DMA((10,)),
            pltpu.SemaphoreType.DMA((10,)),
            pltpu.SemaphoreType.DMA((9,)),
            pltpu.SemaphoreType.REGULAR,
        ],
        compiler_params=pltpu.CompilerParams(
            collective_id=0, has_side_effects=True, vmem_limit_bytes=32 * 2**20
        ),
        name="update",
    )(*operands)
    results = (coeffs, update.reshape(FOWN, D), rest.reshape(NSAMP, 128))
    results = tuple(pltpu.with_memory_space_constraint(a, pltpu.VMEM) for a in results)
    coeffs, update, rest = pl.pallas_call(
        write_out,
        out_shape=tuple(jax.ShapeDtypeStruct(a.shape, a.dtype) for a in results),
        in_specs=[vmem] * 3,
        out_specs=(pl.BlockSpec(memory_space=pltpu.HBM),) * 3,
        scratch_shapes=[pltpu.SemaphoreType.DMA((3,))],
        name="write_out",
    )(*results)
    return (coeffs.reshape(-1), update.T, rest.reshape(-1))


def solution(mesh):
    return jax.shard_map(
        per_device,
        mesh=mesh,
        in_specs=(
            P("samp", None), P(), P(), P(None, "par"), P("par"), P("par"), P("samp", "par"), P(), P(),
        ),
        out_specs=(P("samp"), P(None, "par"), P("par")),
        check_vma=False,
    )
```

```python
import itertools

import jax
import jax.numpy as jnp
from jax import lax
from jax.experimental import pallas as pl
from jax.experimental.pallas import tpu as pltpu
from jax.sharding import PartitionSpec as P

MESH = pl.DeviceIdType.MESH
HI = lax.Precision.HIGHEST
F32 = jnp.float32
BF16 = jnp.bfloat16

LSIDE = 10
PATCHES = 25
D = 64
SAMPLES = 256
OWN = 8
FOWN = 32
NSAMP = 32
NPAR = 8
NX, NZH, NY = 4, 2, 4
PANEL = 16
ROWS = 512


def place():
    samp = lax.axis_index("samp")
    par = lax.axis_index("par")
    x, zh, y = samp // 8, (samp // 4) % 2, samp % 4
    zl, core = par // 2, par % 2
    return samp, par, x, zh, y, zl, core


def site_patch(site):
    line = (site * 205) >> 11
    at = site - line * 10
    return (line >> 1) * 5 + (at >> 1), (line & 1) * 2 + (at & 1)


def patterns(shape, dim):
    pattern = lax.broadcasted_iota(jnp.int32, shape, dim) & 15
    return [jnp.where((pattern >> k) & 1 == 1, 1.0, -1.0) for k in range(4)]


def tables(q, embed_ref, position_ref, weights, table, terms, match):
    for half in (0, D):
        table[0:4, half : half + D] = embed_ref[...]
        table[8 : 8 + PATCHES, half : half + D] = position_ref[...]
    hidden = sum(sign * table[k : k + 1, :] for k, sign in enumerate(patterns((ROWS, 128), 0)))
    hidden += jnp.concatenate(
        [jnp.broadcast_to(table[8 + p : 9 + p, :], (16, 128)) for p in range(PATCHES)]
        + [jnp.zeros((ROWS - 16 * PATCHES, 128), F32)], axis=0
    )
    hidden = hidden.astype(BF16)
    lane = lax.broadcasted_iota(jnp.int32, (1, 128), 1)
    for c in range(2):
        units = jnp.concatenate(
            [jnp.broadcast_to(weights[c, pl.ds(2 * q + n, 1), :], (D, 128)) for n in range(2)], axis=0
        ).astype(BF16)

        def along(row):
            values = weights[c, row : row + 1, :]
            both = [jnp.sum(jnp.where(lane == 2 * q + n, values, 0.0), axis=1, keepdims=True) for n in range(2)]
            return jnp.where(lane < D, both[0], both[1])

        act = lax.dot_general(hidden, units, (((1,), (1,)), ((), ())), preferred_element_type=F32) + along(FOWN)
        rest = hidden.astype(F32) * (along(FOWN + 1) * jnp.tanh(act))
        for n in range(3):
            term = rest.astype(BF16)
            terms[:, 256 * n + 128 * c : 256 * n + 128 * c + 128] = term
            rest = rest - term.astype(F32)
    shape = (128, ROWS)
    patch, place_in = site_patch(lax.broadcasted_iota(jnp.int32, shape, 0))
    signs = patterns(shape, 1)
    sign = jnp.where(
        place_in == 0, signs[0], jnp.where(place_in == 1, signs[1], jnp.where(place_in == 2, signs[2], signs[3]))
    )
    match[...] = jnp.where(patch == lax.broadcasted_iota(jnp.int32, shape, 1) >> 4, sign, 0.0).astype(BF16)


def derivatives(spins_all, terms, match):
    got = spins_all[...].astype(F32)
    spins = jnp.concatenate(
        [
            got[x * 4 + y, 8 * zh : 8 * zh + 8, :]
            for x, zh, y in itertools.product(range(NX), range(NZH), range(NY))
        ], axis=0
    ).astype(BF16)
    score = jnp.dot(spins, match[...], preferred_element_type=F32)
    has = jnp.where(score > 3.5, 1.0, 0.0).astype(BF16)
    grads = jnp.dot(has, terms[...], preferred_element_type=F32)
    return grads[:, 0:256] + (grads[:, 256:512] + grads[:, 512:768])


def offsets():
    def far(step):
        return sum(min(d, 4 - d) for d in step)
    return sorted(filter(any, itertools.product(range(NX), range(NY))), key=far, reverse=True)


def solve(gram_ref, shift, target, upper_ref, scaled_ref, upper_terms, scaled_terms):
    lane = lax.broadcasted_iota(jnp.int32, (8, 128), 1)
    sub = lax.broadcasted_iota(jnp.int32, (8, 128), 0)
    panel_lane = lax.broadcasted_iota(jnp.int32, (PANEL, 128), 1)
    nothing = jnp.zeros((PANEL, 128), BF16)

    def product(left, right):
        return lax.dot_general(left, right, (((0,), (0,)), ((), ())), preferred_element_type=F32)

    tiles = PANEL // 8
    panels = SAMPLES // PANEL
    reach = {}
    for m in range(panels):
        base = PANEL * m
        diag, off = base // 128, base % 128
        for n in (0, 1) if m == 0 else ((m + 1,) if m + 1 < panels else ()):
            first = PANEL * n
            owed = None
            if m:
                right = []
                for term in range(3):
                    halves = []
                    for half in range(2):
                        pieces = []
                        for p in range(m):
                            piece = scaled_terms[term, PANEL * p : PANEL * (p + 1), 128 * half : 128 * half + 128]
                            start = max(0, PANEL * (p + 1) - 128 * half)
                            end = off if half == diag else 128
                            if half <= diag and start < end:
                                piece = jnp.where((panel_lane < start) | (panel_lane >= end), piece, nothing)
                            pieces.append(piece)
                        halves.append(jnp.concatenate(pieces, axis=0))
                    right.append(jnp.concatenate(halves, axis=1))
                left = [upper_terms[term, 0:base, first : first + PANEL] for term in range(3)]
                most = product(jnp.concatenate(left, axis=1), right[0])
                some = product(jnp.concatenate(left[:2], axis=1), right[1])
                least = product(left[0], right[2])
                owed = most[0:16] + (
                    (most[16:32] + some[0:16]) + (some[16:32] + (most[32:48] + least))
                )
            rows = []
            for tile in range(tiles):
                pair = []
                for half in range(2):
                    part = gram_ref[first // PANEL, tile, :, 128 * half : 128 * half + 128]
                    at = first + 8 * tile - 128 * half
                    if 0 <= at < 128:
                        part = jnp.where(lane == sub + at, part + shift, part)
                    if half < diag:
                        part = jnp.zeros_like(part)
                    elif half == diag and off:
                        part = jnp.where(lane >= off, part, 0.0)
                    if owed is not None:
                        part = part - owed[8 * tile : 8 * tile + 8, 128 * half : 128 * half + 128]
                    pair.append(part)
                rows.append(pair)
            reach[n] = rows
        near = [n for n in (m, m + 1) if n < panels]
        inside = (lane >= off) & (lane < off + PANEL)
        column = {}
        for j in range(PANEL):
            for n in near:
                for tile in range(tiles):
                    column[j, n, tile] = jnp.broadcast_to(reach[n][tile][diag][:, off + j : off + j + 1], (8, 128))
        for n in near:
            for tile in range(tiles):
                reach[n][tile][diag] = jnp.where(inside, 0.0, reach[n][tile][diag])
        for j in range(PANEL):
            mine, at = j // 8, j % 8
            inverse = 1.0 / column[j, m, mine][at : at + 1, :]
            live = [
                (n, tile) for n in near for tile in range(tiles)
                if n > m or tile > mine or (tile == mine and at < 7)
            ]
            for k in range(j + 1, PANEL):
                factor = column[k, m, mine][at : at + 1, :] * inverse
                for n, tile in live:
                    column[k, n, tile] = column[k, n, tile] - column[j, n, tile] * factor
            for half in range(2):
                pivot_row = reach[m][mine][half][at : at + 1, :]
                if half == diag:
                    pivot_row = jnp.where(lane[0:1] == off + j, 1.0, pivot_row)
                scaled = pivot_row * inverse
                upper_ref[base + j : base + j + 1, 128 * half : 128 * half + 128] = pivot_row
                scaled_ref[base + j : base + j + 1, 128 * half : 128 * half + 128] = scaled
                for n, tile in live:
                    reach[n][tile][half] = reach[n][tile][half] - column[j, n, tile] * scaled
        for ref, ref_terms in ((upper_ref, upper_terms), (scaled_ref, scaled_terms)):
            rest = ref[base : base + PANEL, :]
            for term in range(3):
                value = rest.astype(BF16)
                ref_terms[term, base : base + PANEL, :] = value
                rest = rest - value.astype(F32)
        del reach[m]
    row = lax.broadcasted_iota(jnp.int32, (SAMPLES, SAMPLES), 0)
    col = lax.broadcasted_iota(jnp.int32, (SAMPLES, SAMPLES), 1)
    low = col <= row
    half_solved = jnp.sum(jnp.where(low, upper_ref[...], 0.0) * target, axis=1, keepdims=True)
    return jnp.sum(jnp.where(low, scaled_ref[...], 0.0) * half_solved, axis=0, keepdims=True)


def center(joined):
    mean = jnp.sum(joined, axis=0, keepdims=True) / SAMPLES
    return ((joined - mean) * 0.0625).astype(BF16)


def kernel(
    spins_hbm, other_hbm, embed_hbm, position_hbm, w_hbm, bias_hbm, readout_hbm, energies_hbm, shift_hbm,
    coeffs_ref, update_ref, rest_ref,
    spins_ref, other_ref, embed_ref, position_ref, w_ref, bias_ref, readout_ref, energies_ref, shift_ref,
    spin_pad, table, weights, terms, match, spin_tile, spin_mirror, spins_all, sbuf, rbuf, cbuf,
    gram_part, plane_in, z_in, gram_ref, upper, scaled, upper_terms, scaled_terms, x_buf, result, results, send_sem, recv_sem, load_sem, ready,
):
    samp, par, x, zh, y, zl, core = place()
    q = x * 4 + y
    z = zh * 4 + zl
    lead = core == 1
    follow = jnp.logical_not(lead)
    summing = jnp.logical_and(lead, zh == 0)
    idle = jnp.logical_and(lead, zh == 1)

    def device(nq, nzh, nzl, ncore):
        return ((nq // 4) * 8 + nzh * 4 + nq % 4, nzl * 2 + ncore)

    def beside(step):
        return lax.rem(x + step[0], 4) * 4 + lax.rem(y + step[1], 4)

    def along_z(nz):
        return device(q, nz // 4, nz % 4, 1)

    def send(src, dst, n, to):
        pltpu.make_async_remote_copy(
            src_ref=src, dst_ref=dst, send_sem=send_sem.at[n], recv_sem=recv_sem.at[n], device_id=to, device_id_type=MESH
        ).start()

    def came(part, n):
        pltpu.make_async_copy(part, part, recv_sem.at[n]).wait()

    def left(part, n):
        pltpu.make_async_copy(part, part, send_sem.at[n]).wait()

    plane = offsets()
    mate = device(q, zh, zl, 1 - core)
    mirror = device(q, 1 - zh, zl, 1)

    barrier = pltpu.get_barrier_semaphore()

    def greet(to):
        pl.semaphore_signal(barrier, inc=1, device_id=to, device_id_type=MESH)

    @pl.when(summing)
    def _():
        for step in plane + [(0, 0)]:
            for c in (0, 1):
                greet(device(beside(step), 1, zl, c))
        for k in (3, 5, 2, 6, 1, 7):
            greet(along_z(lax.rem(z + k, 8)))
        for step in plane:
            for c in (0, 1):
                greet(device(beside(step), 0, zl, c))

    @pl.when(idle)
    def _():
        for step in plane:
            greet(device(beside(step), 1, zl, 1))

    @pl.when(follow)
    def _():
        for step in plane:
            greet(device(beside(step), zh, zl, 1))

    greet(mate)

    loads = [
        pltpu.make_async_copy(a, b, load_sem.at[n])
        for n, (a, b) in enumerate(
            (
                (spins_hbm, spins_ref), (other_hbm, other_ref), (embed_hbm, embed_ref), (position_hbm, position_ref),
                (w_hbm, w_ref), (bias_hbm, bias_ref), (readout_hbm, readout_ref),
                (energies_hbm, energies_ref), (shift_hbm, shift_ref),
            )
        )
    ]
    for load in loads:
        load.start()
    for load in loads:
        load.wait()
    spin_pad[...] = jnp.zeros_like(spin_pad)
    spin_pad[:, 0:100] = spins_ref[...].astype(F32)
    spin_tile[...] = jnp.concatenate([spin_pad[...], jnp.zeros((8, 128), F32)], axis=0).astype(BF16)
    for n in range(16):
        sbuf[n] = jnp.concatenate(
            [other_ref[:, 128 * m : 128 * m + 128].astype(F32) for m in (2 * n, 2 * n + 1)], axis=0
        ).astype(BF16)
    weights[core] = jnp.zeros((40, 128), F32)
    weights[core, 0:FOWN, 0:D] = w_ref[...].astype(F32)
    weights[core, FOWN : FOWN + 1, 0:FOWN] = bias_ref[...]
    weights[core, FOWN + 1 : FOWN + 2, 0:FOWN] = readout_ref[...]

    def share(step):
        nq = beside(step)
        send(sbuf.at[nq], rbuf.at[core * NSAMP + samp], 0, device(nq, 0, zl, 1))

    @pl.when(summing)
    def _():
        pl.semaphore_wait(barrier, 34)
        for step in plane:
            share(step)

    @pl.when(idle)
    def _():
        pl.semaphore_wait(barrier, 50)
        send(spin_tile, spin_mirror, 6, mirror)
        for step in plane + [(0, 0)]:
            share(step)
        for nz in range(4):
            pl.semaphore_signal(ready, inc=1, device_id=along_z(nz), device_id_type=MESH)

    @pl.when(jnp.logical_and(follow, zh == 0))
    def _():
        pl.semaphore_wait(barrier, 16)
        for step in plane + [(0, 0)]:
            share(step)
        send(weights.at[0], weights.at[0], 8, mate)

    @pl.when(jnp.logical_and(follow, zh == 1))
    def _():
        pl.semaphore_wait(barrier, 17)
        for step in plane + [(0, 0)]:
            share(step)

    @pl.when(summing)
    def _():
        came(weights.at[0], 8)
        tables(q, embed_ref, position_ref, weights, table, terms, match)
        rbuf[NSAMP + samp] = sbuf[q]
        came(spin_mirror, 6)
        spins_all[q] = jnp.concatenate([spin_pad[...], spin_mirror[...].astype(F32)[0:8, :]], axis=0).astype(BF16)
        for step in plane:
            send(spins_all.at[q], spins_all.at[q], 7, device(beside(step), 0, zl, 1))
        came(spins_all.at[pl.ds(0, 15)], 7)
        cbuf[:, 512:768] = center(derivatives(spins_all, terms, match))

        def products(columns):
            return lax.dot_general(columns, columns, (((1,), (1,)), ((), ())), preferred_element_type=F32)

        gram_part[...] = products(cbuf[:, 512:768]).reshape(16, 2, 8, SAMPLES)
        came(rbuf.at[pl.ds(0, 2 * NSAMP - 1)], 0)
        for c in range(2):
            got = rbuf[NSAMP * c : NSAMP * (c + 1)].astype(F32)
            for n in range(2):
                at = 256 * c + 128 * n
                cbuf[:, at : at + 128] = center(got[:, 8 * n : 8 * n + 8, :].reshape(SAMPLES, 128))

        gram_part[...] += products(cbuf[:, 0:512]).reshape(16, 2, 8, SAMPLES)
        for step in plane:
            nq = beside(step)
            send(gram_part.at[nq], plane_in.at[q], 1, device(nq, 0, zl, 1))
        plane_in[q] = gram_part[q]
        came(plane_in.at[pl.ds(0, 15)], 1)
        z_in[zl] = jnp.sum(plane_in[...], axis=0)

        pl.semaphore_wait(ready, 4)
        for k in (4, 3, 5, 2, 6, 1, 7):
            send(z_in.at[zl], z_in.at[zl], 2, along_z(lax.rem(z + k, 8)))
        came(z_in.at[pl.ds(0, 3)], 2)
        send(cbuf, cbuf, 5, mirror)

    @pl.when(idle)
    def _():
        came(z_in, 2)

    @pl.when(lead)
    def _():
        gram_ref[q] = jnp.sum(z_in[...], axis=0)
        for step in plane:
            send(gram_ref.at[q], gram_ref.at[q], 3, device(beside(step), zh, zl, 1))
        energies = energies_ref[...]
        target = energies - jnp.sum(energies, axis=1, keepdims=True) / SAMPLES
        came(gram_ref.at[pl.ds(0, 15)], 3)

        x_row = solve(gram_ref, shift_ref[...], target, upper, scaled, upper_terms, scaled_terms)
        x_buf[...] = jnp.broadcast_to(x_row, (8, SAMPLES))
        send(x_buf, x_buf, 9, mate)

        @pl.when(zh == 1)
        def _():
            came(cbuf, 5)

        first = x_row.astype(BF16).astype(F32)
        second = (x_row - first).astype(BF16).astype(F32)
        split = jnp.concatenate(
            [first, second, x_row - first - second, jnp.zeros((13, SAMPLES), F32)], axis=0
        ).astype(BF16)
        full = jnp.dot(split, cbuf[...], preferred_element_type=F32)
        full = full[0:1] + (full[1:2] + full[2:3])
        result[...] = jnp.zeros_like(result)
        for n, (c, row) in enumerate(((0, 0), (0, 1), (1, 0), (1, 1), (0, 2), (1, 2))):
            result[c, row : row + 1, :] = full[:, 128 * n : 128 * n + 128]
        for step in plane:
            send(result.at[1], results.at[q], 4, device(beside(step), zh, zl, 1))
        for step in plane + [(0, 0)]:
            send(result.at[0], results.at[q], 4, device(beside(step), zh, zl, 0))
        results[q] = result[1]
        came(results.at[pl.ds(0, 15)], 4)

    @pl.when(follow)
    def _():
        came(x_buf, 9)
        came(results, 4)

    coeffs_ref[...] = pltpu.roll(x_buf[...], lax.rem(SAMPLES - OWN * samp, SAMPLES), 1)[0:1, 0:OWN]
    rest_ref[...] = results[:, 0:2, :]
    layer = results[:, 2, :]
    update_ref[:, 0, :] = layer[:, 0:D]
    update_ref[:, 1, :] = pltpu.roll(layer, D, 1)[:, 0:D]

    @pl.when(lead)
    def _():
        for part, n in ((gram_ref.at[pl.ds(0, 15)], 3), (results, 4), (results.at[pl.ds(0, 15)], 4), (x_buf, 9)):
            left(part, n)

    @pl.when(summing)
    def _():
        for part, n in (
            (rbuf.at[pl.ds(0, 15)], 0), (plane_in.at[pl.ds(0, 15)], 1), (plane_in.at[pl.ds(0, 7)], 2), (cbuf, 5),
            (spins_all.at[pl.ds(0, 15)], 7),
        ):
            left(part, n)

    @pl.when(jnp.logical_not(summing))
    def _():
        left(rbuf.at[pl.ds(0, 16)], 0)

    @pl.when(idle)
    def _():
        left(spin_tile, 6)

    @pl.when(jnp.logical_and(follow, zh == 0))
    def _():
        left(weights.at[0], 8)


def write_out(coeffs, update, rest, coeffs_out, update_out, rest_out, sem):
    copies = [
        pltpu.make_async_copy(a, b, sem.at[n])
        for n, (a, b) in enumerate(((rest, rest_out), (update, update_out), (coeffs, coeffs_out)))
    ]
    for copy in copies:
        copy.start()
    for copy in copies:
        copy.wait()


def per_device(spins, embed, position, w_first, bias_first, readout, other_grads, energies, shift):
    vmem = pl.BlockSpec(memory_space=pltpu.VMEM)
    operands = (
        spins, other_grads, embed, position, w_first.T, bias_first.reshape(1, -1), readout.reshape(1, -1),
        energies.reshape(1, -1), shift.reshape(1, 1),
    )
    operands = tuple(pltpu.with_memory_space_constraint(a, pltpu.HBM) for a in operands[:-1]) + operands[-1:]
    coeffs, update, rest = pl.pallas_call(
        kernel,
        out_shape=(
            jax.ShapeDtypeStruct((1, OWN), F32),
            jax.ShapeDtypeStruct((16, 2, D), F32),
            jax.ShapeDtypeStruct((16, 2, 128), F32),
        ),
        in_specs=[pl.BlockSpec(memory_space=pltpu.HBM)] * 9,
        out_specs=(vmem,) * 3,
        scratch_shapes=[pltpu.VMEM(a.shape, a.dtype) for a in operands]
        + [
            pltpu.VMEM((8, 128), F32),
            pltpu.VMEM((40, 128), F32),
            pltpu.VMEM((2, 40, 128), F32),
            pltpu.VMEM((ROWS, 768), BF16),
            pltpu.VMEM((128, ROWS), BF16),
            pltpu.VMEM((16, 128), BF16),
            pltpu.VMEM((16, 128), BF16),
            pltpu.VMEM((16, 16, 128), BF16),
            pltpu.VMEM((16, 16, 128), BF16),
            pltpu.VMEM((2 * NSAMP, 16, 128), BF16),
            pltpu.VMEM((SAMPLES, 768), BF16),
            pltpu.VMEM((16, 2, 8, SAMPLES), F32),
            pltpu.VMEM((16, 2, 8, SAMPLES), F32),
            pltpu.VMEM((4, 2, 8, SAMPLES), F32),
            pltpu.VMEM((16, 2, 8, SAMPLES), F32),
            pltpu.VMEM((SAMPLES, SAMPLES), F32),
            pltpu.VMEM((SAMPLES, SAMPLES), F32),
            pltpu.VMEM((3, SAMPLES, SAMPLES), BF16),
            pltpu.VMEM((3, SAMPLES, SAMPLES), BF16),
            pltpu.VMEM((8, SAMPLES), F32),
            pltpu.VMEM((2, 4, 128), F32),
            pltpu.VMEM((16, 4, 128), F32),
            pltpu.SemaphoreType.DMA((10,)),
            pltpu.SemaphoreType.DMA((10,)),
            pltpu.SemaphoreType.DMA((9,)),
            pltpu.SemaphoreType.REGULAR,
        ],
        compiler_params=pltpu.CompilerParams(
            collective_id=0, has_side_effects=True, vmem_limit_bytes=32 * 2**20
        ),
        name="update",
    )(*operands)
    results = (coeffs, update.reshape(FOWN, D), rest.reshape(NSAMP, 128))
    results = tuple(pltpu.with_memory_space_constraint(a, pltpu.VMEM) for a in results)
    coeffs, update, rest = pl.pallas_call(
        write_out,
        out_shape=tuple(jax.ShapeDtypeStruct(a.shape, a.dtype) for a in results),
        in_specs=[vmem] * 3,
        out_specs=(pl.BlockSpec(memory_space=pltpu.HBM),) * 3,
        scratch_shapes=[pltpu.SemaphoreType.DMA((3,))],
        name="write_out",
    )(*results)
    return (coeffs.reshape(-1), update.T, rest.reshape(-1))


def solution(mesh):
    return jax.shard_map(
        per_device,
        mesh=mesh,
        in_specs=(
            P("samp", None), P(), P(), P(None, "par"), P("par"), P("par"), P("samp", "par"), P(), P(),
        ),
        out_specs=(P("samp"), P(None, "par"), P("par")),
        check_vma=False,
    )
```

```python
import itertools

import jax
import jax.numpy as jnp
from jax import lax
from jax.experimental import pallas as pl
from jax.experimental.pallas import tpu as pltpu
from jax.sharding import PartitionSpec as P

MESH = pl.DeviceIdType.MESH
HI = lax.Precision.HIGHEST
F32 = jnp.float32
BF16 = jnp.bfloat16

LSIDE = 10
PATCHES = 25
D = 64
SAMPLES = 256
OWN = 8
FOWN = 32
NSAMP = 32
NPAR = 8
NX, NZH, NY = 4, 2, 4
PANEL = 16
ROWS = 512


def place():
    samp = lax.axis_index("samp")
    par = lax.axis_index("par")
    x, zh, y = samp // 8, (samp // 4) % 2, samp % 4
    zl, core = par // 2, par % 2
    return samp, par, x, zh, y, zl, core


def site_patch(site):
    line = (site * 205) >> 11
    at = site - line * 10
    return (line >> 1) * 5 + (at >> 1), (line & 1) * 2 + (at & 1)


def patterns(shape, dim):
    pattern = lax.broadcasted_iota(jnp.int32, shape, dim) & 15
    return [jnp.where((pattern >> k) & 1 == 1, 1.0, -1.0) for k in range(4)]


def tables(q, embed_ref, position_ref, weights, table, terms, match):
    for half in (0, D):
        table[0:4, half : half + D] = embed_ref[...]
        table[8 : 8 + PATCHES, half : half + D] = position_ref[...]
    hidden = sum(sign * table[k : k + 1, :] for k, sign in enumerate(patterns((ROWS, 128), 0)))
    hidden += jnp.concatenate(
        [jnp.broadcast_to(table[8 + p : 9 + p, :], (16, 128)) for p in range(PATCHES)]
        + [jnp.zeros((ROWS - 16 * PATCHES, 128), F32)], axis=0
    )
    hidden = hidden.astype(BF16)
    lane = lax.broadcasted_iota(jnp.int32, (1, 128), 1)
    for c in range(2):
        units = jnp.concatenate(
            [jnp.broadcast_to(weights[c, pl.ds(2 * q + n, 1), :], (D, 128)) for n in range(2)], axis=0
        ).astype(BF16)

        def along(row):
            values = weights[c, row : row + 1, :]
            both = [jnp.sum(jnp.where(lane == 2 * q + n, values, 0.0), axis=1, keepdims=True) for n in range(2)]
            return jnp.where(lane < D, both[0], both[1])

        act = lax.dot_general(hidden, units, (((1,), (1,)), ((), ())), preferred_element_type=F32) + along(FOWN)
        rest = hidden.astype(F32) * (along(FOWN + 1) * jnp.tanh(act))
        for n in range(3):
            term = rest.astype(BF16)
            terms[:, 256 * n + 128 * c : 256 * n + 128 * c + 128] = term
            rest = rest - term.astype(F32)
    shape = (128, ROWS)
    patch, place_in = site_patch(lax.broadcasted_iota(jnp.int32, shape, 0))
    signs = patterns(shape, 1)
    sign = jnp.where(
        place_in == 0, signs[0], jnp.where(place_in == 1, signs[1], jnp.where(place_in == 2, signs[2], signs[3]))
    )
    match[...] = jnp.where(patch == lax.broadcasted_iota(jnp.int32, shape, 1) >> 4, sign, 0.0).astype(BF16)


def derivatives(spins_all, terms, match):
    got = spins_all[...].astype(F32)
    spins = jnp.concatenate(
        [
            got[n, 0:8, :] for n in range(NSAMP)
        ], axis=0
    ).astype(BF16)
    score = jnp.dot(spins, match[...], preferred_element_type=F32)
    has = jnp.where(score > 3.5, 1.0, 0.0).astype(BF16)
    grads = jnp.dot(has, terms[...], preferred_element_type=F32)
    return grads[:, 0:256] + (grads[:, 256:512] + grads[:, 512:768])


def offsets():
    def far(step):
        return sum(min(d, 4 - d) for d in step)
    return sorted(filter(any, itertools.product(range(NX), range(NY))), key=far, reverse=True)


def solve(gram_ref, shift, target, upper_ref, scaled_ref, upper_terms, scaled_terms):
    lane = lax.broadcasted_iota(jnp.int32, (8, 128), 1)
    sub = lax.broadcasted_iota(jnp.int32, (8, 128), 0)
    panel_lane = lax.broadcasted_iota(jnp.int32, (PANEL, 128), 1)
    nothing = jnp.zeros((PANEL, 128), BF16)

    def product(left, right):
        return lax.dot_general(left, right, (((0,), (0,)), ((), ())), preferred_element_type=F32)

    tiles = PANEL // 8
    panels = SAMPLES // PANEL
    reach = {}
    for m in range(panels):
        base = PANEL * m
        diag, off = base // 128, base % 128
        for n in (0, 1) if m == 0 else ((m + 1,) if m + 1 < panels else ()):
            first = PANEL * n
            owed = None
            if m:
                right = []
                for term in range(3):
                    halves = []
                    for half in range(2):
                        pieces = []
                        for p in range(m):
                            piece = scaled_terms[term, PANEL * p : PANEL * (p + 1), 128 * half : 128 * half + 128]
                            start = max(0, PANEL * (p + 1) - 128 * half)
                            end = off if half == diag else 128
                            if half <= diag and start < end:
                                piece = jnp.where((panel_lane < start) | (panel_lane >= end), piece, nothing)
                            pieces.append(piece)
                        halves.append(jnp.concatenate(pieces, axis=0))
                    right.append(jnp.concatenate(halves, axis=1))
                left = [upper_terms[term, 0:base, first : first + PANEL] for term in range(3)]
                most = product(jnp.concatenate(left, axis=1), right[0])
                some = product(jnp.concatenate(left[:2], axis=1), right[1])
                least = product(left[0], right[2])
                owed = most[0:16] + (
                    (most[16:32] + some[0:16]) + (some[16:32] + (most[32:48] + least))
                )
            rows = []
            for tile in range(tiles):
                pair = []
                for half in range(2):
                    part = gram_ref[first // PANEL, tile, :, 128 * half : 128 * half + 128]
                    at = first + 8 * tile - 128 * half
                    if 0 <= at < 128:
                        part = jnp.where(lane == sub + at, part + shift, part)
                    if half < diag:
                        part = jnp.zeros_like(part)
                    elif half == diag and off:
                        part = jnp.where(lane >= off, part, 0.0)
                    if owed is not None:
                        part = part - owed[8 * tile : 8 * tile + 8, 128 * half : 128 * half + 128]
                    pair.append(part)
                rows.append(pair)
            reach[n] = rows
        near = [n for n in (m, m + 1) if n < panels]
        inside = (lane >= off) & (lane < off + PANEL)
        column = {}
        for j in range(PANEL):
            for n in near:
                for tile in range(tiles):
                    column[j, n, tile] = jnp.broadcast_to(reach[n][tile][diag][:, off + j : off + j + 1], (8, 128))
        for n in near:
            for tile in range(tiles):
                reach[n][tile][diag] = jnp.where(inside, 0.0, reach[n][tile][diag])
        for j in range(PANEL):
            mine, at = j // 8, j % 8
            inverse = 1.0 / column[j, m, mine][at : at + 1, :]
            live = [
                (n, tile) for n in near for tile in range(tiles)
                if n > m or tile > mine or (tile == mine and at < 7)
            ]
            for k in range(j + 1, PANEL):
                factor = column[k, m, mine][at : at + 1, :] * inverse
                for n, tile in live:
                    column[k, n, tile] = column[k, n, tile] - column[j, n, tile] * factor
            for half in range(2):
                pivot_row = reach[m][mine][half][at : at + 1, :]
                if half == diag:
                    pivot_row = jnp.where(lane[0:1] == off + j, 1.0, pivot_row)
                scaled = pivot_row * inverse
                upper_ref[base + j : base + j + 1, 128 * half : 128 * half + 128] = pivot_row
                scaled_ref[base + j : base + j + 1, 128 * half : 128 * half + 128] = scaled
                for n, tile in live:
                    reach[n][tile][half] = reach[n][tile][half] - column[j, n, tile] * scaled
        for ref, ref_terms in ((upper_ref, upper_terms), (scaled_ref, scaled_terms)):
            rest = ref[base : base + PANEL, :]
            for term in range(3):
                value = rest.astype(BF16)
                ref_terms[term, base : base + PANEL, :] = value
                rest = rest - value.astype(F32)
        del reach[m]
    row = lax.broadcasted_iota(jnp.int32, (SAMPLES, SAMPLES), 0)
    col = lax.broadcasted_iota(jnp.int32, (SAMPLES, SAMPLES), 1)
    low = col <= row
    half_solved = jnp.sum(jnp.where(low, upper_ref[...], 0.0) * target, axis=1, keepdims=True)
    return jnp.sum(jnp.where(low, scaled_ref[...], 0.0) * half_solved, axis=0, keepdims=True)


def center(joined):
    mean = jnp.sum(joined, axis=0, keepdims=True) / SAMPLES
    return ((joined - mean) * 0.0625).astype(BF16)


def kernel(
    spins_hbm, other_hbm, embed_hbm, position_hbm, w_hbm, bias_hbm, readout_hbm, energies_hbm, shift_hbm,
    coeffs_ref, update_ref, rest_ref,
    spins_ref, other_ref, embed_ref, position_ref, w_ref, bias_ref, readout_ref, energies_ref, shift_ref,
    spin_pad, table, weights, terms, match, spin_tile, spins_all, sbuf, rbuf, cbuf,
    gram_part, plane_in, z_in, gram_ref, upper, scaled, upper_terms, scaled_terms, x_buf, result, results, send_sem, recv_sem, load_sem, ready,
):
    samp, par, x, zh, y, zl, core = place()
    q = x * 4 + y
    z = zh * 4 + zl
    lead = core == 1
    follow = jnp.logical_not(lead)
    summing = jnp.logical_and(lead, zh == 0)
    idle = jnp.logical_and(lead, zh == 1)

    def device(nq, nzh, nzl, ncore):
        return ((nq // 4) * 8 + nzh * 4 + nq % 4, nzl * 2 + ncore)

    def beside(step):
        return lax.rem(x + step[0], 4) * 4 + lax.rem(y + step[1], 4)

    def along_z(nz):
        return device(q, nz // 4, nz % 4, 1)

    def send(src, dst, n, to):
        pltpu.make_async_remote_copy(
            src_ref=src, dst_ref=dst, send_sem=send_sem.at[n], recv_sem=recv_sem.at[n], device_id=to, device_id_type=MESH
        ).start()

    def came(part, n):
        pltpu.make_async_copy(part, part, recv_sem.at[n]).wait()

    def left(part, n):
        pltpu.make_async_copy(part, part, send_sem.at[n]).wait()

    plane = offsets()
    mate = device(q, zh, zl, 1 - core)
    mirror = device(q, 1 - zh, zl, 1)

    barrier = pltpu.get_barrier_semaphore()

    def greet(to):
        pl.semaphore_signal(barrier, inc=1, device_id=to, device_id_type=MESH)

    @pl.when(summing)
    def _():
        for step in plane + [(0, 0)]:
            for c in (0, 1):
                greet(device(beside(step), 1, zl, c))
        for k in (3, 5, 2, 6, 1, 7):
            greet(along_z(lax.rem(z + k, 8)))
        for step in plane:
            for c in (0, 1):
                greet(device(beside(step), 0, zl, c))
        greet(mate)

    loads = [
        pltpu.make_async_copy(a, b, load_sem.at[n])
        for n, (a, b) in enumerate(
            (
                (spins_hbm, spins_ref), (other_hbm, other_ref), (embed_hbm, embed_ref), (position_hbm, position_ref),
                (w_hbm, w_ref), (bias_hbm, bias_ref), (readout_hbm, readout_ref),
                (energies_hbm, energies_ref), (shift_hbm, shift_ref),
            )
        )
    ]
    for load in loads:
        load.start()
    for load in loads:
        load.wait()
    spin_pad[...] = jnp.zeros_like(spin_pad)
    spin_pad[:, 0:100] = spins_ref[...].astype(F32)
    spin_tile[...] = jnp.concatenate([spin_pad[...], jnp.zeros((8, 128), F32)], axis=0).astype(BF16)
    for n in range(16):
        sbuf[n] = jnp.concatenate(
            [other_ref[:, 128 * m : 128 * m + 128].astype(F32) for m in (2 * n, 2 * n + 1)], axis=0
        ).astype(BF16)
    weights[core] = jnp.zeros((40, 128), F32)
    weights[core, 0:FOWN, 0:D] = w_ref[...].astype(F32)
    weights[core, FOWN : FOWN + 1, 0:FOWN] = bias_ref[...]
    weights[core, FOWN + 1 : FOWN + 2, 0:FOWN] = readout_ref[...]

    def show(step):
        send(spin_tile, spins_all.at[samp], 7, device(beside(step), 0, zl, 1))

    def share(step):
        nq = beside(step)
        send(sbuf.at[nq], rbuf.at[core * NSAMP + samp], 0, device(nq, 0, zl, 1))

    @pl.when(summing)
    def _():
        pl.semaphore_wait(barrier, 18)
        for step in plane:
            share(step)
            show(step)

    @pl.when(idle)
    def _():
        pl.semaphore_wait(barrier, 19)
        for step in plane + [(0, 0)]:
            share(step)
        for nz in range(4):
            pl.semaphore_signal(ready, inc=1, device_id=along_z(nz), device_id_type=MESH)

    @pl.when(jnp.logical_and(follow, zh == 0))
    def _():
        pl.semaphore_wait(barrier, 16)
        for step in plane + [(0, 0)]:
            share(step)
        send(weights.at[0], weights.at[0], 8, mate)

    @pl.when(jnp.logical_and(follow, zh == 1))
    def _():
        pl.semaphore_wait(barrier, 16)
        for step in plane + [(0, 0)]:
            show(step)
            share(step)

    @pl.when(summing)
    def _():
        came(weights.at[0], 8)
        tables(q, embed_ref, position_ref, weights, table, terms, match)
        rbuf[NSAMP + samp] = sbuf[q]
        spins_all[samp] = spin_tile[...]
        came(spins_all.at[pl.ds(0, 31)], 7)
        cbuf[:, 512:768] = center(derivatives(spins_all, terms, match))

        def products(columns):
            return lax.dot_general(columns, columns, (((1,), (1,)), ((), ())), preferred_element_type=F32)

        gram_part[...] = products(cbuf[:, 512:768]).reshape(16, 2, 8, SAMPLES)
        came(rbuf.at[pl.ds(0, 2 * NSAMP - 1)], 0)
        for c in range(2):
            got = rbuf[NSAMP * c : NSAMP * (c + 1)].astype(F32)
            for n in range(2):
                at = 256 * c + 128 * n
                cbuf[:, at : at + 128] = center(got[:, 8 * n : 8 * n + 8, :].reshape(SAMPLES, 128))

        gram_part[...] += products(cbuf[:, 0:512]).reshape(16, 2, 8, SAMPLES)
        for step in plane:
            nq = beside(step)
            send(gram_part.at[nq], plane_in.at[q], 1, device(nq, 0, zl, 1))
        plane_in[q] = gram_part[q]
        came(plane_in.at[pl.ds(0, 15)], 1)
        z_in[zl] = jnp.sum(plane_in[...], axis=0)

        pl.semaphore_wait(ready, 4)
        for k in (4, 3, 5, 2, 6, 1, 7):
            send(z_in.at[zl], z_in.at[zl], 2, along_z(lax.rem(z + k, 8)))
        came(z_in.at[pl.ds(0, 3)], 2)
        send(cbuf, cbuf, 5, mirror)

    @pl.when(idle)
    def _():
        came(z_in, 2)

    @pl.when(lead)
    def _():
        gram_ref[q] = jnp.sum(z_in[...], axis=0)
        for step in plane:
            send(gram_ref.at[q], gram_ref.at[q], 3, device(beside(step), zh, zl, 1))
        energies = energies_ref[...]
        target = energies - jnp.sum(energies, axis=1, keepdims=True) / SAMPLES
        came(gram_ref.at[pl.ds(0, 15)], 3)

        x_row = solve(gram_ref, shift_ref[...], target, upper, scaled, upper_terms, scaled_terms)
        x_buf[...] = jnp.broadcast_to(x_row, (8, SAMPLES))
        send(x_buf, x_buf, 9, mate)

        @pl.when(zh == 1)
        def _():
            came(cbuf, 5)

        first = x_row.astype(BF16).astype(F32)
        second = (x_row - first).astype(BF16).astype(F32)
        split = jnp.concatenate(
            [first, second, x_row - first - second, jnp.zeros((13, SAMPLES), F32)], axis=0
        ).astype(BF16)
        full = jnp.dot(split, cbuf[...], preferred_element_type=F32)
        full = full[0:1] + (full[1:2] + full[2:3])
        result[...] = jnp.zeros_like(result)
        for n, (c, row) in enumerate(((0, 0), (0, 1), (1, 0), (1, 1), (0, 2), (1, 2))):
            result[c, row : row + 1, :] = full[:, 128 * n : 128 * n + 128]
        for step in plane:
            send(result.at[1], results.at[q], 4, device(beside(step), zh, zl, 1))
        for step in plane + [(0, 0)]:
            send(result.at[0], results.at[q], 4, device(beside(step), zh, zl, 0))
        results[q] = result[1]
        came(results.at[pl.ds(0, 15)], 4)

    @pl.when(follow)
    def _():
        came(x_buf, 9)
        came(results, 4)

    coeffs_ref[...] = pltpu.roll(x_buf[...], lax.rem(SAMPLES - OWN * samp, SAMPLES), 1)[0:1, 0:OWN]
    rest_ref[...] = results[:, 0:2, :]
    layer = results[:, 2, :]
    update_ref[:, 0, :] = layer[:, 0:D]
    update_ref[:, 1, :] = pltpu.roll(layer, D, 1)[:, 0:D]

    @pl.when(lead)
    def _():
        for part, n in ((gram_ref.at[pl.ds(0, 15)], 3), (results, 4), (results.at[pl.ds(0, 15)], 4), (x_buf, 9)):
            left(part, n)

    @pl.when(summing)
    def _():
        for part, n in (
            (rbuf.at[pl.ds(0, 15)], 0), (plane_in.at[pl.ds(0, 15)], 1), (plane_in.at[pl.ds(0, 7)], 2), (cbuf, 5),
            (spins_all.at[pl.ds(0, 15)], 7),
        ):
            left(part, n)

    @pl.when(jnp.logical_not(summing))
    def _():
        left(rbuf.at[pl.ds(0, 16)], 0)

    @pl.when(jnp.logical_and(follow, zh == 1))
    def _():
        left(spins_all.at[pl.ds(0, 16)], 7)

    @pl.when(jnp.logical_and(follow, zh == 0))
    def _():
        left(weights.at[0], 8)


def write_out(coeffs, update, rest, coeffs_out, update_out, rest_out, sem):
    copies = [
        pltpu.make_async_copy(a, b, sem.at[n])
        for n, (a, b) in enumerate(((rest, rest_out), (update, update_out), (coeffs, coeffs_out)))
    ]
    for copy in copies:
        copy.start()
    for copy in copies:
        copy.wait()


def per_device(spins, embed, position, w_first, bias_first, readout, other_grads, energies, shift):
    vmem = pl.BlockSpec(memory_space=pltpu.VMEM)
    operands = (
        spins, other_grads, embed, position, w_first.T, bias_first.reshape(1, -1), readout.reshape(1, -1),
        energies.reshape(1, -1), shift.reshape(1, 1),
    )
    operands = tuple(pltpu.with_memory_space_constraint(a, pltpu.HBM) for a in operands[:-1]) + operands[-1:]
    coeffs, update, rest = pl.pallas_call(
        kernel,
        out_shape=(
            jax.ShapeDtypeStruct((1, OWN), F32),
            jax.ShapeDtypeStruct((16, 2, D), F32),
            jax.ShapeDtypeStruct((16, 2, 128), F32),
        ),
        in_specs=[pl.BlockSpec(memory_space=pltpu.HBM)] * 9,
        out_specs=(vmem,) * 3,
        scratch_shapes=[pltpu.VMEM(a.shape, a.dtype) for a in operands]
        + [
            pltpu.VMEM((8, 128), F32),
            pltpu.VMEM((40, 128), F32),
            pltpu.VMEM((2, 40, 128), F32),
            pltpu.VMEM((ROWS, 768), BF16),
            pltpu.VMEM((128, ROWS), BF16),
            pltpu.VMEM((16, 128), BF16),
            pltpu.VMEM((NSAMP, 16, 128), BF16),
            pltpu.VMEM((16, 16, 128), BF16),
            pltpu.VMEM((2 * NSAMP, 16, 128), BF16),
            pltpu.VMEM((SAMPLES, 768), BF16),
            pltpu.VMEM((16, 2, 8, SAMPLES), F32),
            pltpu.VMEM((16, 2, 8, SAMPLES), F32),
            pltpu.VMEM((4, 2, 8, SAMPLES), F32),
            pltpu.VMEM((16, 2, 8, SAMPLES), F32),
            pltpu.VMEM((SAMPLES, SAMPLES), F32),
            pltpu.VMEM((SAMPLES, SAMPLES), F32),
            pltpu.VMEM((3, SAMPLES, SAMPLES), BF16),
            pltpu.VMEM((3, SAMPLES, SAMPLES), BF16),
            pltpu.VMEM((8, SAMPLES), F32),
            pltpu.VMEM((2, 4, 128), F32),
            pltpu.VMEM((16, 4, 128), F32),
            pltpu.SemaphoreType.DMA((10,)),
            pltpu.SemaphoreType.DMA((10,)),
            pltpu.SemaphoreType.DMA((9,)),
            pltpu.SemaphoreType.REGULAR,
        ],
        compiler_params=pltpu.CompilerParams(
            collective_id=0, has_side_effects=True, vmem_limit_bytes=32 * 2**20
        ),
        name="update",
    )(*operands)
    results = (coeffs, update.reshape(FOWN, D), rest.reshape(NSAMP, 128))
    results = tuple(pltpu.with_memory_space_constraint(a, pltpu.VMEM) for a in results)
    coeffs, update, rest = pl.pallas_call(
        write_out,
        out_shape=tuple(jax.ShapeDtypeStruct(a.shape, a.dtype) for a in results),
        in_specs=[vmem] * 3,
        out_specs=(pl.BlockSpec(memory_space=pltpu.HBM),) * 3,
        scratch_shapes=[pltpu.SemaphoreType.DMA((3,))],
        name="write_out",
    )(*results)
    return (coeffs.reshape(-1), update.T, rest.reshape(-1))


def solution(mesh):
    return jax.shard_map(
        per_device,
        mesh=mesh,
        in_specs=(
            P("samp", None), P(), P(), P(None, "par"), P("par"), P("par"), P("samp", "par"), P(), P(),
        ),
        out_specs=(P("samp"), P(None, "par"), P("par")),
        check_vma=False,
    )
```
